32 devices in a mesh: groups: 2 (over y), tile: 4 (over z), shot: 4 (over x, core).
Axes of the slice: x: 2, y: 2, z: 4, core: 2. Of those that a mesh axis runs over, the one named last changes fastest.
Arguments:
- velocity: bfloat16 [64, 64, 128], P(('groups', 'tile')), parts along dimension 0, may hold values from 0.25 to 0.3984375
- epsilon: bfloat16 [64, 64, 128], P(('groups', 'tile')), parts along dimension 0, may hold values from 0 to 0.29882812
- delta: bfloat16 [64, 64, 128], P(('groups', 'tile')), parts along dimension 0, may hold values from -0.049804688 to 0.19921875
- tilt: bfloat16 [64, 64, 128], P(('groups', 'tile')), parts along dimension 0, may hold values from -0.8984375 to 0.8984375
- forward_state: float32 [8, 2, 32, 64, 128], P(('groups', 'shot'), None, 'tile'), parts along dimension 0, may hold values from -2 to 2
- adjoint_state: float32 [8, 2, 32, 64, 128], P(('groups', 'shot'), None, 'tile'), parts along dimension 0, may hold values from -2 to 2
- offsets: int32 [8], P(('groups', 'shot')), parts along dimension 0, may hold values from 0 to 31
- src_cells: int32 [8], P(('groups', 'shot')), parts along dimension 0, may hold values from 0 to 262143
- rec_cells: int32 [8, 128], P(('groups', 'shot')), parts along dimension 0, may hold values from 0 to 262143, as said below
- wavelet: float32 [8, 4], P(('groups', 'shot')), parts along dimension 0, may hold values from -4 to 4
- observed: float32 [8, 4, 128], P(('groups', 'shot')), parts along dimension 0, may hold values from -5 to 5
Outputs:
- grad_velocity: float32 [64, 64, 128], P(('groups', 'tile'), 'shot'), parts along dimension 0
- grad_epsilon: float32 [64, 64, 128], P(('groups', 'tile'), 'shot'), parts along dimension 0
- grad_delta: float32 [64, 64, 128], P(('groups', 'tile'), 'shot'), parts along dimension 0
The draws below stay inside these ranges and needn't reach their ends.
There are 2 independent parts, one for each index of `groups`. The reference program is written for one: setup_inputs(seed, part) draws one part's arguments, and reference() takes and returns one part's arrays. A program takes and returns all parts, laid end to end along the dimension named above; each array names one. Nothing has to cross between parts.
Inputs may be any that keep to these rules, and one draw needn't show every extreme that they name: `rec_cells`: a flat index x * 64 * 128 + y * 128 + z into the shot's aperture grid; in every shot some receivers share their cell with another receiver of that shot. `src_cells`: a flat index into the shot's aperture grid, as for the receivers.
All inputs are finite; a program needn't handle non-finite values.
Results may differ from the reference program's by a relative error of at most 0.0003.
Values may be sent and summed in bfloat16 or wider, within the bound.
No kernel may reach another device: no remote copies, remote signals or barrier semaphores. Data moves between devices by JAX's collectives and lax.ppermute only.
A program may use at most 64 MiB of HBM per device.

```python
import jax
import jax.numpy as jnp

NY = 64
NZ = 128
NT = 4
NREC = 128
NX = 32
SHOTS = 4


def draw_rec_cells(key, part):
    key = jax.random.fold_in(key, 7)
    key_cells, key_pick, key_partner, key_first = jax.random.split(key, 4)
    cells = jax.random.randint(key_cells, (SHOTS, NREC), 0, NX * NY * NZ)
    partner = jax.random.randint(key_partner, (SHOTS, NREC), 0, NREC)
    chosen = jax.random.randint(key_pick, (SHOTS, NREC), 0, 8) == 0
    column = jnp.arange(NREC)[None, :]
    copied = jnp.take_along_axis(cells, partner, axis=1)
    rest = jnp.where(chosen & (column > 0), copied, cells)
    first_partner = jax.random.randint(key_first, (SHOTS, 1), 1, NREC)
    first_cell = jnp.take_along_axis(rest, first_partner, axis=1)
    result = jnp.where(column == 0, first_cell, rest)
    return result.astype(jnp.int32)


def place_ends(array, own_key, least, top_value):
    longest = array.shape.index(max(array.shape))
    spots = []
    for shift in (0, 1):
        where = [jax.random.randint(jax.random.fold_in(own_key, axis), (), 0, length) for axis, length in enumerate(array.shape)]
        where[longest] = (where[longest] + shift) % array.shape[longest]
        spots.append(tuple(where))
    return array.at[spots[0]].set(least).at[spots[1]].set(top_value)


def levels(key, shape, pieces, low, top_value):
    level = 1.0
    for position, parts in pieces:
        draws = jax.random.uniform(jax.random.fold_in(jax.random.fold_in(key, 6), position), (parts,), jnp.float32, low / len(pieces), top_value / len(pieces))
        level = level * jnp.repeat(jnp.exp(draws), shape[position] // parts).reshape((-1,) + (1,) * (len(shape) - 1 - position))
    return level


def bell_draw(stream_key, extent, scale, most, cuts=(), kind=jnp.bfloat16):
    factor_of = levels(stream_key, extent, cuts, -0.22, 0.18) if cuts else 1.0
    drawn = jax.random.normal(stream_key, extent, jnp.float32) * scale * factor_of
    return jnp.minimum(jnp.maximum(drawn, -most), most).astype(kind)


def setup_inputs(seed: int = 0, part: int = 0) -> dict:
    key_of = jax.random.split(jax.random.key(seed), 12)
    part_keys = jax.random.split(jax.random.fold_in(key_of[11], part), 12)
    return {
        "velocity": jnp.clip(0.25 + 0.1484375 * jax.random.uniform(part_keys[0], (NX, NY, NZ), jnp.float32) ** levels(part_keys[0], (NX, NY, NZ), ((0, 4),), -0.2, 0.2), 0.25, 0.3984375).astype(jnp.bfloat16),
        "epsilon": jnp.clip(0.29882812 * jax.random.uniform(part_keys[1], (NX, NY, NZ), jnp.float32) ** levels(part_keys[1], (NX, NY, NZ), ((0, 4),), -0.2, 0.2), 0.0, 0.29882812).astype(jnp.bfloat16),
        "delta": jnp.clip(-0.049804688 + 0.24902344 * jax.random.uniform(part_keys[2], (NX, NY, NZ), jnp.float32) ** levels(part_keys[2], (NX, NY, NZ), ((0, 4),), -0.2, 0.2), -0.049804688, 0.19921875).astype(jnp.bfloat16),
        "tilt": jnp.clip(jax.random.uniform(part_keys[3], (NX, NY, NZ), jnp.float32, -0.8984375, 0.8984375) * levels(part_keys[3], (NX, NY, NZ), ((0, 4),), -0.4, 0.0), -0.8984375, 0.8984375).astype(jnp.bfloat16),
        "forward_state": bell_draw(part_keys[4], (SHOTS, 2, NX, NY, NZ), 0.3, 2.0, ((0, 4), (2, 4)), jnp.float32),
        "adjoint_state": bell_draw(part_keys[5], (SHOTS, 2, NX, NY, NZ), 0.3, 2.0, ((0, 4), (2, 4)), jnp.float32),
        "offsets": place_ends(jax.random.randint(part_keys[6], (SHOTS,), 0, NX), jax.random.fold_in(part_keys[6], 1), 0, NX - 1).astype(jnp.int32),
        "src_cells": place_ends(jax.random.randint(part_keys[7], (SHOTS,), 0, NX * NY * NZ), jax.random.fold_in(part_keys[7], 1), 0, (NX * NY * NZ) - 1).astype(jnp.int32),
        "rec_cells": draw_rec_cells(jax.random.fold_in(jax.random.fold_in(key_of[11], part), 71), part),
        "wavelet": bell_draw(part_keys[9], (SHOTS, NT), 1.0, 4.0, ((0, 4),), jnp.float32),
        "observed": bell_draw(part_keys[10], (SHOTS, NT, NREC), 1.0, 5.0, ((0, 4),), jnp.float32),
    }


def extend(field):
    return jnp.concatenate([field[-1:], field, field[:1]], axis=0)


def second(ext):
    padded = jnp.pad(ext, ((0, 0), (1, 1), (1, 1)))
    centre = padded[1:-1, 1:-1, 1:-1]
    dxx = padded[2:, 1:-1, 1:-1] - 2.0 * centre + padded[:-2, 1:-1, 1:-1]
    dyy = padded[1:-1, 2:, 1:-1] - 2.0 * centre + padded[1:-1, :-2, 1:-1]
    dzz = padded[1:-1, 1:-1, 2:] - 2.0 * centre + padded[1:-1, 1:-1, :-2]
    dxz = 0.25 * (padded[2:, 1:-1, 2:] - padded[2:, 1:-1, :-2] - padded[:-2, 1:-1, 2:] + padded[:-2, 1:-1, :-2])
    return dxx, dyy, dzz, dxz


def vertical(ext, sine, cosine):
    dxx, dyy, dzz, dxz = second(ext)
    return sine * sine * dxx + cosine * cosine * dzz + 2.0 * sine * cosine * dxz


def horizontal(ext, sine, cosine):
    dxx, dyy, dzz, dxz = second(ext)
    vert = sine * sine * dxx + cosine * cosine * dzz + 2.0 * sine * cosine * dxz
    return dxx + dyy + dzz - vert


def add_at(field, cells, values):
    return field.reshape(-1).at[cells].add(values).reshape(field.shape)


def reference(velocity, epsilon, delta, tilt, forward_state, adjoint_state, offsets, src_cells, rec_cells, wavelet, observed):
    total_v = jnp.zeros((NX, NY, NZ), jnp.float32)
    total_e = jnp.zeros((NX, NY, NZ), jnp.float32)
    total_d = jnp.zeros((NX, NY, NZ), jnp.float32)
    for shot_id in range(SHOTS):
        offset = offsets[shot_id]
        speed = jnp.roll(velocity.astype(jnp.float32), -offset, axis=0)
        eps_a = jnp.roll(epsilon.astype(jnp.float32), -offset, axis=0)
        del_a = jnp.roll(delta.astype(jnp.float32), -offset, axis=0)
        tilt_a = jnp.roll(tilt.astype(jnp.float32), -offset, axis=0)
        vsq = speed * speed
        gain_e = 1.0 + 2.0 * eps_a
        gain_d = 1.0 + 2.0 * del_a
        sine = jnp.sin(tilt_a)
        cosine = jnp.cos(tilt_a)
        source = jnp.reshape(src_cells[shot_id], (1,))
        receivers = rec_cells[shot_id]
        press = forward_state[shot_id, 0]
        shear = forward_state[shot_id, 1]
        press_old, shear_old = press, shear
        stored = []
        records = []
        for step in range(NT):
            hor_p = horizontal(extend(press), sine, cosine)
            ver_q = vertical(extend(shear), sine, cosine)
            press_new = 2.0 * press - press_old + vsq * (gain_e * hor_p + ver_q)
            shear_new = 2.0 * shear - shear_old + vsq * (gain_d * hor_p + ver_q)
            amount = jnp.reshape(wavelet[shot_id, step], (1,))
            press_new = add_at(press_new, source, amount)
            shear_new = add_at(shear_new, source, amount)
            records.append(press_new.reshape(-1)[receivers])
            stored.append((hor_p, ver_q))
            press_old, press, shear_old, shear = press, press_new, shear, shear_new
        residual_data = jnp.stack(records) - observed[shot_id]
        lam = adjoint_state[shot_id, 0]
        mu = adjoint_state[shot_id, 1]
        lam_old, mu_old = lam, mu
        grad_v = jnp.zeros_like(lam)
        grad_e = jnp.zeros_like(lam)
        grad_d = jnp.zeros_like(lam)
        for step in range(NT - 1, -1, -1):
            first_w = vsq * (gain_e * lam + gain_d * mu)
            second_w = vsq * (lam + mu)
            lam_new = 2.0 * lam - lam_old + horizontal(extend(first_w), sine, cosine)
            mu_new = 2.0 * mu - mu_old + vertical(extend(second_w), sine, cosine)
            lam_new = add_at(lam_new, receivers, residual_data[step])
            hor_p, ver_q = stored[step]
            grad_v = grad_v + 2.0 * speed * (lam_new * (gain_e * hor_p + ver_q) + mu_new * (gain_d * hor_p + ver_q))
            grad_e = grad_e + 2.0 * vsq * lam_new * hor_p
            grad_d = grad_d + 2.0 * vsq * mu_new * hor_p
            lam_old, lam, mu_old, mu = lam, lam_new, mu, mu_new
        total_v = total_v + jnp.roll(grad_v, offset, axis=0)
        total_e = total_e + jnp.roll(grad_e, offset, axis=0)
        total_d = total_d + jnp.roll(grad_d, offset, axis=0)
    return total_v, total_e, total_d
```

```python
import functools

import jax
import jax.numpy as jnp
from jax import lax
from jax.experimental import pallas as pl
from jax.experimental.pallas import tpu as pltpu
from jax.sharding import PartitionSpec as P

TOP = 32767.0
PAD = 8
STATE_BOUND = 2.0


def passed_along(x, axis, by):
    count = lax.axis_size(axis)
    return lax.ppermute(x, axis, [(i, (i + by) % count) for i in range(count)])


def swapped(x, mask):
    count = lax.axis_size("shot")
    return lax.ppermute(x, "shot", [(i, i ^ mask) for i in range(count)])


def encoded(x, inverse):
    root = jnp.sqrt(jnp.sqrt(jnp.abs(x) * inverse))
    level = jnp.minimum(root * TOP + 0.5, TOP)
    return jnp.where(x < 0, -level, level).astype(jnp.int32).astype(jnp.int16)


def decoded(code, scale):
    level = code.astype(jnp.int32).astype(jnp.float32) * (1.0 / TOP)
    square = level * level
    value = square * square * scale
    return jnp.where(level < 0, -value, value)


def vmem(count):
    return [pl.BlockSpec(memory_space=pltpu.VMEM)] * count


def smem(count):
    return [pl.BlockSpec(memory_space=pltpu.SMEM)] * count


def anywhere(count):
    return [pl.BlockSpec(memory_space=pl.ANY)] * count


def edges_kernel(fwd_wide, adj_wide, fwd, adj, f_up, f_down, a_up, a_down):
    rows = fwd.shape[2]
    inverse = 1.0 / STATE_BOUND
    for state, up, down, wide in ((fwd, f_up, f_down, fwd_wide), (adj, a_up, a_down, adj_wide)):
        for field in range(2):

            @pl.loop(0, wide)
            def _(i):
                up[field, i] = encoded(state[0, field, rows - wide + i], inverse)
                down[field, i] = encoded(state[0, field, i], inverse)


def receivers_kernel(steps, ext, rows, tiles, rec, observed, out):
    span, ny, nz = out.shape[1:]
    count = rec.shape[1]
    nx = rows * tiles
    first = lax.axis_index("tile") * rows - ext
    cells = rec[...]
    plane = ny * nz
    x = cells // plane - first
    x = jnp.where(x < 0, x + nx, x)
    x = jnp.where(x >= nx, x - nx, x)
    line = x * ny + (cells // nz) % ny
    depth = cells % nz
    hit = (lax.broadcasted_iota(jnp.int32, (span * ny, count), 0) == line).astype(jnp.float32)
    column = lax.broadcasted_iota(jnp.int32, (nz, count), 0) == depth
    for k in range(steps + 1):
        value = observed[0, pl.ds(k - 1, 1), :] if k else jnp.ones((1, count), jnp.float32)
        weights = jnp.where(column, value, 0.0)
        dense = lax.dot_general(
            hit,
            weights,
            (((1,), (1,)), ((), ())),
            precision=lax.Precision.HIGHEST,
            preferred_element_type=jnp.float32,
        )
        out[k] = dense.reshape(span, ny, nz)


def sin_cos(t):
    u = t * t
    s = 1.0 / 6227020800.0
    for c in (-1.0 / 39916800.0, 1.0 / 362880.0, -1.0 / 5040.0, 1.0 / 120.0, -1.0 / 6.0, 1.0):
        s = s * u + c
    s = s * t
    c = 1.0 / 479001600.0
    for d in (-1.0 / 3628800.0, 1.0 / 40320.0, -1.0 / 720.0, 1.0 / 24.0, -0.5, 1.0):
        c = c * u + d
    return s, c


def waves_kernel(cfg, *refs):
    steps, ext, near, tiles, coded, n_model = cfg
    it = iter(refs)
    offset_ref, source_ref, wavelet_ref = next(it), next(it), next(it)
    model_refs = [next(it) for _ in range(n_model)]
    fwd, adj, f_lo, f_hi, a_lo, a_hi, dense = (next(it) for _ in range(7))
    outs = [next(it) for _ in range(4 if coded else 1)]
    (model, press, shear, kept_h, kept_v, lam, mu, w1, w2, vsq, ge, gd, s2, sc, grads, dense_v,
     f_code, a_code, sem_model, sem_f, sem_a, sem_d) = it

    rows, ny, nz = fwd.shape[2:]
    total = rows + 2 * ext
    inner = slice(PAD, PAD + ny)
    up_one = slice(PAD - 1, PAD + ny - 1)
    down_one = slice(PAD + 1, PAD + ny + 1)
    span = rows + 2 * near
    low = ext - near
    wide = steps
    low_a = ext - wide

    f_copies = [
        pltpu.make_async_copy(fwd.at[0, 0], press.at[0, pl.ds(ext, rows), pl.ds(PAD, ny)], sem_f),
        pltpu.make_async_copy(fwd.at[0, 1], shear.at[0, pl.ds(ext, rows)], sem_f),
        pltpu.make_async_copy(f_lo, f_code.at[0], sem_f),
        pltpu.make_async_copy(f_hi, f_code.at[1], sem_f),
    ]
    m_copies = []
    if coded:
        j = lax.axis_index("shot")
        for index, ref in enumerate(model_refs):
            if index < 4:
                target = model.at[index, 0]
            else:
                rel, mask = (index - 4) // 4 + 1, (index - 4) % 4
                target = model.at[j ^ mask, rel]
            m_copies.append(pltpu.make_async_copy(ref, target, sem_model))
    else:
        for rel, ref in enumerate(model_refs):
            for field in range(4):
                m_copies.append(pltpu.make_async_copy(ref.at[field], model.at[field, rel], sem_model))
    a_copies = [
        pltpu.make_async_copy(adj.at[0, 0], lam.at[0, pl.ds(ext, rows)], sem_a),
        pltpu.make_async_copy(adj.at[0, 1], mu.at[0, pl.ds(ext, rows)], sem_a),
        pltpu.make_async_copy(a_lo, a_code.at[0], sem_a),
        pltpu.make_async_copy(a_hi, a_code.at[1], sem_a),
    ]
    d_copy = pltpu.make_async_copy(dense, dense_v, sem_d)
    for copy in m_copies + f_copies + a_copies + [d_copy]:
        copy.start()

    edge = jnp.zeros((PAD, nz), jnp.float32)

    @pl.loop(0, total)
    def _(i):
        for k in range(steps):
            press[k, i, 0:PAD] = edge
            press[k, i, PAD + ny:] = edge
        w1[i, 0:PAD] = edge
        w1[i, PAD + ny:] = edge

    for copy in m_copies:
        copy.wait()
    offset = offset_ref[0]
    around = rows * 4

    @pl.loop(1, total - 1)
    def _(i):
        at = (i - ext + offset + around) % around
        tile, row = at // rows, at % rows
        va = model[0, tile, row].astype(jnp.float32)
        sine, cosine = sin_cos(model[3, tile, row].astype(jnp.float32))
        vsq[i] = va * va
        ge[i] = 1.0 + 2.0 * model[1, tile, row].astype(jnp.float32)
        gd[i] = 1.0 + 2.0 * model[2, tile, row].astype(jnp.float32)
        s2[i] = sine * sine
        sc[i] = 0.5 * sine * cosine

    lane = lax.broadcasted_iota(jnp.int32, (ny, nz), 1)
    not_first, not_last = lane > 0, lane < nz - 1

    def depth_terms(centre, diff, a, b):
        upper = a * pltpu.roll(centre, nz - 1, 1) + b * pltpu.roll(diff, nz - 1, 1)
        lower = a * pltpu.roll(centre, 1, 1) - b * pltpu.roll(diff, 1, 1)
        return jnp.where(not_last, upper, 0.0) + jnp.where(not_first, lower, 0.0)

    def flat(low_row, centre, high_row, up, down, a2, ab):
        side = low_row + high_row
        diff = high_row - low_row
        return (side - a2 * side) + (up + down) - 4.0 * centre + depth_terms(centre, diff, a2, -ab)

    def steep(low_row, centre, high_row, a2, ab):
        side = low_row + high_row
        diff = high_row - low_row
        return a2 * side - 2.0 * centre + depth_terms(centre, diff, 1.0 - a2, ab)

    for copy in f_copies:
        copy.wait()

    @pl.loop(0, ext)
    def _(i):
        for side, base in ((0, 0), (1, ext + rows)):
            press[0, base + i, inner] = decoded(f_code[side, 0, i], STATE_BOUND)
            shear[0, base + i] = decoded(f_code[side, 1, i], STATE_BOUND)

    tile_first = lax.axis_index("tile") * rows
    nx = rows * tiles
    cell = source_ref[0]
    src_row = (cell // (ny * nz) - tile_first + ext + nx) % nx
    src_y = (cell // nz) % ny
    src_here = lax.broadcasted_iota(jnp.int32, (1, nz), 1) == cell % nz

    for k in range(steps):
        now, new = k % 2, (k + 1) % 2

        def forward_row(i, keep):
            p = press[k, i, inner]
            q = shear[now, i]
            a2, ab = s2[i], sc[i]
            hp = flat(press[k, i - 1, inner], p, press[k, i + 1, inner],
                      press[k, i, up_one], press[k, i, down_one], a2, ab)
            hq = steep(shear[now, i - 1], q, shear[now, i + 1], a2, ab)
            if keep:
                kept_h[k, i - ext] = hp
                kept_v[k, i - ext] = hq
            speed = vsq[i]
            p_base = 2.0 * p - press[k - 1, i, inner] if k else p
            q_base = 2.0 * q - shear[new, i] if k else q
            press[k + 1, i, inner] = p_base + speed * (ge[i] * hp + hq)
            shear[new, i] = q_base + speed * (gd[i] * hp + hq)

        pl.loop(1 + k, ext)(lambda i: forward_row(i, False))
        pl.loop(ext, ext + rows)(lambda i: forward_row(i, True))
        pl.loop(ext + rows, total - 1 - k)(lambda i: forward_row(i, False))

        @pl.when((src_row >= 1 + k) & (src_row < total - 1 - k))
        def _():
            amount = jnp.where(src_here, wavelet_ref[0, k], 0.0)
            press[k + 1, src_row, pl.ds(PAD + src_y, 1)] += amount
            shear[new, src_row, pl.ds(src_y, 1)] += amount

    for copy in a_copies:
        copy.wait()

    @pl.loop(0, wide)
    def _(i):
        for side, base in ((0, low_a), (1, ext + rows)):
            lam[0, base + i] = decoded(a_code[side, 0, i], STATE_BOUND)
            mu[0, base + i] = decoded(a_code[side, 1, i], STATE_BOUND)

    d_copy.wait()
    for a in range(steps):
        k = steps - 1 - a
        now, new = a % 2, (a + 1) % 2

        @pl.loop(low_a + a, total - low_a - a)
        def _(i):
            l, m = lam[now, i], mu[now, i]
            speed = vsq[i]
            w1[i, inner] = speed * (ge[i] * l + gd[i] * m)
            w2[i] = speed * (l + m)

        def adjoint_row(i, inside):
            a2, ab = s2[i], sc[i]
            h = flat(w1[i - 1, inner], w1[i, inner], w1[i + 1, inner], w1[i, up_one], w1[i, down_one], a2, ab)
            v = steep(w2[i - 1], w2[i], w2[i + 1], a2, ab)
            l, m = lam[now, i], mu[now, i]
            l_base = 2.0 * l - lam[new, i] if a else l
            m_base = 2.0 * m - mu[new, i] if a else m
            residual = dense_v[0, i - low] * press[k + 1, i, inner] - dense_v[k + 1, i - low]
            l_new = l_base + h + residual
            m_new = m_base + v
            if a < steps - 1:
                lam[new, i] = l_new
                mu[new, i] = m_new
            if inside:
                r = i - ext
                hp, hq = kept_h[k, r], kept_v[k, r]
                sums = (l_new * hp, m_new * hp, (l_new + m_new) * hq)
                if a:
                    sums = tuple(grads[n, r] + sums[n] for n in range(3))
                if a == steps - 1:
                    at = (i - ext + offset + around) % around
                    twice = 2.0 * model[0, at // rows, at % rows].astype(jnp.float32)
                    twice_sq = 2.0 * vsq[i]
                    sums = (
                        twice * (ge[i] * sums[0] + gd[i] * sums[1] + sums[2]),
                        twice_sq * sums[0],
                        twice_sq * sums[1],
                    )
                for n in range(3):
                    grads[n, r] = sums[n]

        if a < steps - 1:
            pl.loop(low_a + a + 1, ext)(lambda i: adjoint_row(i, False))
        pl.loop(ext, ext + rows)(lambda i: adjoint_row(i, True))
        if a < steps - 1:
            pl.loop(ext + rows, total - low_a - a - 1)(lambda i: adjoint_row(i, False))

    if not coded:
        outs[0][...] = grads[...]
        return
    quarter = ny // 4
    scales = []
    for n in range(3):
        top = jnp.max(jnp.max(jnp.abs(grads[n]), axis=0), axis=0, keepdims=True)
        top = jnp.maximum(jnp.max(top, axis=1, keepdims=True), 1e-30)
        scales.append(jnp.broadcast_to(jnp.ceil(jnp.log2(top)) + 1.0, (quarter, nz)))
    for mask in range(4):
        y0 = pl.multiple_of((j ^ mask) * quarter, quarter)
        for n in range(3):
            inverse = jnp.exp2(-scales[n])

            @pl.loop(0, rows)
            def _(r):
                part = grads[n, r, pl.ds(y0, quarter)]
                if mask:
                    outs[mask][n * rows + r] = encoded(part, inverse)
                else:
                    outs[0][n * rows + r] = part

            if mask:
                outs[mask][3 * rows + 1 + n] = scales[n].astype(jnp.int32).astype(jnp.int16)
        if mask:
            outs[mask][3 * rows] = jnp.full((quarter, nz), offset, jnp.int32).astype(jnp.int16)


def gather_kernel(rows, offset_ref, own, *refs):
    codes, (here, *outs), acc = refs[:3], refs[3:7], refs[7]
    around = 4 * rows
    quarter, nz = own.shape[1:]
    zero = jnp.zeros((quarter, nz), jnp.float32)

    @pl.loop(0, around)
    def _(x):
        for n in range(3):
            acc[n, x] = zero

    offset = offset_ref[0]

    @pl.loop(0, rows)
    def _(r):
        for n in range(3):
            acc[n, (r + offset) % around] += own[n * rows + r]

    for code in codes:
        theirs = jnp.max(code[3 * rows].astype(jnp.int32).astype(jnp.float32)).astype(jnp.int32)
        scale = [jnp.exp2(code[3 * rows + 1 + n].astype(jnp.int32).astype(jnp.float32)) for n in range(3)]

        @pl.loop(0, rows)
        def _(r):
            for n in range(3):
                acc[n, (r + theirs) % around] += decoded(code[n * rows + r], scale[n])

    for n in range(3):
        here[pl.ds(n * rows, rows)] = acc[n, pl.ds(0, rows)]
    for rel in range(1, 4):
        out = outs[rel - 1]
        for n in range(3):
            top = jnp.max(jnp.abs(acc[n, pl.ds(rel * rows, rows)]), axis=0)
            top = jnp.max(top, axis=0, keepdims=True)
            top = jnp.maximum(jnp.max(top, axis=1, keepdims=True), 1e-30)
            power = jnp.broadcast_to(jnp.ceil(jnp.log2(top)) + 1.0, (quarter, nz))
            inverse = jnp.exp2(-power)

            @pl.loop(0, rows)
            def _(r):
                out[n * rows + r] = encoded(acc[n, rel * rows + r], inverse)

            out[3 * rows + n] = power.astype(jnp.int32).astype(jnp.int16)


def finish_kernel(rows, own, *refs):
    codes, outs = refs[:3], refs[3:]
    for n in range(3):
        scale = [jnp.exp2(code[3 * rows + n].astype(jnp.int32).astype(jnp.float32)) for code in codes]

        @pl.loop(0, rows)
        def _(r):
            total = own[n * rows + r]
            for code, s in zip(codes, scale):
                total = total + decoded(code[n * rows + r], s)
            outs[n][r] = total


def on_device(
    velocity,
    epsilon,
    delta,
    tilt,
    forward_state,
    adjoint_state,
    offsets,
    src_cells,
    rec_cells,
    wavelet,
    observed,
):
    rows, ny, nz = velocity.shape
    tiles = lax.axis_size("tile")
    shots = lax.axis_size("shot")
    steps = wavelet.shape[1]
    ext = 2 * steps - 1
    near = steps - 1
    total = rows + 2 * ext
    span = rows + 2 * near
    assert rows >= ext
    coded = tiles == 4 and shots == 4
    f32, i16 = jnp.float32, jnp.int16

    def edges(width):
        return jax.ShapeDtypeStruct((2, width, ny, nz), i16)

    if coded:
        j = lax.axis_index("shot")
        quarter_field = lax.select_n(j, velocity, epsilon, delta, tilt)
        ahead = passed_along(quarter_field, "tile", -1)
        behind = passed_along(quarter_field, "tile", 1)
        across = passed_along(quarter_field, "tile", 2)
        model_refs = [velocity, epsilon, delta, tilt]
        for piece in (ahead, across, behind):
            other = swapped(piece, 2)
            model_refs += [piece, swapped(piece, 1), other, swapped(other, 1)]
        shift = offsets
    else:
        nbits = max(1, (tiles - 1).bit_length())
        block = jnp.stack([velocity, epsilon, delta, tilt])
        whole = offsets[0] // rows
        for bit in range(nbits):
            moved = passed_along(block, "tile", -(1 << bit))
            block = jnp.where(jnp.bitwise_and(jnp.right_shift(whole, bit), 1) == 1, moved, block)
        model_refs = [block] + [passed_along(block, "tile", -by) for by in (1, 2, -1)]
        shift = offsets % rows

    f_up, f_down, a_up, a_down = pl.pallas_call(
        functools.partial(edges_kernel, ext, steps),
        out_shape=[edges(ext), edges(ext), edges(steps), edges(steps)],
        in_specs=vmem(2),
        out_specs=vmem(4),
        name="edges",
    )(forward_state, adjoint_state)
    f_lo = passed_along(f_up, "tile", 1)
    f_hi = passed_along(f_down, "tile", -1)
    a_lo = passed_along(a_up, "tile", 1)
    a_hi = passed_along(a_down, "tile", -1)

    dense = pl.pallas_call(
        functools.partial(receivers_kernel, steps, near, rows, tiles),
        out_shape=jax.ShapeDtypeStruct((steps + 1, span, ny, nz), f32),
        in_specs=vmem(2),
        out_specs=pl.BlockSpec(memory_space=pltpu.VMEM),
        compiler_params=pltpu.CompilerParams(vmem_limit_bytes=32 * 1024 * 1024),
        name="receivers",
    )(rec_cells, observed)

    quarter = ny // 4
    if coded:
        slab = jax.ShapeDtypeStruct((3 * rows + 4, quarter, nz), i16)
        wave_outs = [jax.ShapeDtypeStruct((3 * rows, quarter, nz), f32), slab, slab, slab]
    else:
        wave_outs = [jax.ShapeDtypeStruct((3, rows, ny, nz), f32)]
    field = (total, ny, nz)
    scratch = [
        pltpu.VMEM((4, 4, rows, ny, nz), jnp.bfloat16),
        pltpu.VMEM((steps + 1, total, ny + 2 * PAD, nz), f32),
        pltpu.VMEM((2,) + field, f32),
        pltpu.VMEM((steps, rows, ny, nz), f32),
        pltpu.VMEM((steps, rows, ny, nz), f32),
        pltpu.VMEM((2,) + field, f32),
        pltpu.VMEM((2,) + field, f32),
        pltpu.VMEM((total, ny + 2 * PAD, nz), f32),
        pltpu.VMEM(field, f32),
        *[pltpu.VMEM(field, f32) for _ in range(5)],
        pltpu.VMEM((3, rows, ny, nz), f32),
        pltpu.VMEM((steps + 1, span, ny, nz), f32),
        pltpu.VMEM((2, 2, ext, ny, nz), i16),
        pltpu.VMEM((2, 2, steps, ny, nz), i16),
        *[pltpu.SemaphoreType.DMA for _ in range(4)],
    ]
    waves = pl.pallas_call(
        functools.partial(waves_kernel, (steps, ext, near, tiles, coded, len(model_refs))),
        out_shape=wave_outs,
        in_specs=smem(3) + anywhere(len(model_refs) + 7),
        out_specs=vmem(len(wave_outs)),
        scratch_shapes=scratch,
        compiler_params=pltpu.CompilerParams(vmem_limit_bytes=48 * 1024 * 1024),
        name="waves",
    )(shift, src_cells, wavelet, *model_refs, forward_state, adjoint_state, f_lo, f_hi, a_lo, a_hi, dense)

    if not coded:
        (gradients,) = waves
        within = shift[0]
        spread = jnp.zeros((3, 2 * rows, ny, nz), f32)
        spread = lax.dynamic_update_slice_in_dim(spread, gradients, within, 1)
        combined = spread[:, :rows] + passed_along(spread[:, rows:], "tile", 1)
        for bit in range(nbits):
            moved = passed_along(combined, "tile", 1 << bit)
            combined = jnp.where(jnp.bitwise_and(jnp.right_shift(whole, bit), 1) == 1, moved, combined)
        summed = lax.psum(combined, "shot")
        share = ny // shots
        result = lax.dynamic_slice_in_dim(summed, lax.axis_index("shot") * share, share, 2)
        return (result[0], result[1], result[2])

    own, *sent = waves
    received = [swapped(code, mask) for mask, code in zip((1, 2, 3), sent)]
    part = jax.ShapeDtypeStruct((3 * rows + 3, quarter, nz), i16)
    here, *parts = pl.pallas_call(
        functools.partial(gather_kernel, rows),
        out_shape=[jax.ShapeDtypeStruct((3 * rows, quarter, nz), f32), part, part, part],
        in_specs=smem(1) + vmem(4),
        out_specs=vmem(4),
        scratch_shapes=[pltpu.VMEM((3, 4 * rows, quarter, nz), f32)],
        name="gather",
    )(offsets, own, *received)
    arrived = [passed_along(p, "tile", rel) for rel, p in zip((1, 2, 3), parts)]
    return tuple(
        pl.pallas_call(
            functools.partial(finish_kernel, rows),
            out_shape=[jax.ShapeDtypeStruct((rows, quarter, nz), f32)] * 3,
            in_specs=vmem(4),
            out_specs=vmem(3),
            name="finish",
        )(here, *arrived)
    )


def solution(mesh):
    placed = (
        P(("groups", "tile"), None, None),
        P(("groups", "tile"), None, None),
        P(("groups", "tile"), None, None),
        P(("groups", "tile"), None, None),
        P(("groups", "shot"), None, "tile", None, None),
        P(("groups", "shot"), None, "tile", None, None),
        P(("groups", "shot")),
        P(("groups", "shot")),
        P(("groups", "shot"), None),
        P(("groups", "shot"), None),
        P(("groups", "shot"), None, None),
    )
    return jax.shard_map(
        on_device,
        mesh=mesh,
        in_specs=placed,
        out_specs=(
            P(("groups", "tile"), "shot", None),
            P(("groups", "tile"), "shot", None),
            P(("groups", "tile"), "shot", None),
        ),
        check_vma=False,
    )
```

```python
import functools

import jax
import jax.numpy as jnp
from jax import lax
from jax.experimental import pallas as pl
from jax.experimental.pallas import tpu as pltpu
from jax.sharding import PartitionSpec as P

TOP = 32767.0
PAD = 8
UNROLL = 4
STATE_BOUND = 2.0


def passed_along(x, axis, by):
    count = lax.axis_size(axis)
    return lax.ppermute(x, axis, [(i, (i + by) % count) for i in range(count)])


def swapped(x, mask):
    count = lax.axis_size("shot")
    return lax.ppermute(x, "shot", [(i, i ^ mask) for i in range(count)])


def encoded(x, inverse):
    root = jnp.sqrt(jnp.sqrt(jnp.abs(x) * inverse))
    level = jnp.minimum(root * TOP + 0.5, TOP)
    return jnp.where(x < 0, -level, level).astype(jnp.int32).astype(jnp.int16)


def decoded(code, scale):
    level = code.astype(jnp.int32).astype(jnp.float32) * (1.0 / TOP)
    square = level * level
    value = square * square * scale
    return jnp.where(level < 0, -value, value)


def power_of(blocks):
    top = functools.reduce(jnp.maximum, [jnp.max(jnp.abs(x), axis=0) for x in blocks])
    top = jnp.max(jnp.max(top, axis=0, keepdims=True), axis=1, keepdims=True)
    return jnp.ceil(jnp.log2(jnp.maximum(top, 1e-30))) + 1.0


def head_row(powers, lines, offset):
    line = lax.broadcasted_iota(jnp.int32, (lines, 128), 0)
    head = jnp.full((lines, 128), offset, jnp.int32)
    for n, power in enumerate(powers):
        head = jnp.where(line == n, jnp.broadcast_to(power, (lines, 128)).astype(jnp.int32), head)
    return head.astype(jnp.int16)


def scales_of(head):
    return [jnp.exp2(head[n:n + 1]) for n in range(3)]


def tiled(x):
    return x.reshape(x.shape[:-2] + (x.shape[-2] // 8, 8, x.shape[-1]))


def vmem(count):
    return [pl.BlockSpec(memory_space=pltpu.VMEM)] * count


def smem(count):
    return [pl.BlockSpec(memory_space=pltpu.SMEM)] * count


def anywhere(count):
    return [pl.BlockSpec(memory_space=pl.ANY)] * count


def edges_kernel(wide, state, up, down):
    rows = state.shape[2]

    @pl.loop(0, wide, unroll=2)
    def _(i):
        for field in range(2):
            up[field, i] = encoded(state[0, field, rows - wide + i], 1.0 / STATE_BOUND)
            down[field, i] = encoded(state[0, field, i], 1.0 / STATE_BOUND)


def receivers_kernel(steps, ext, rows, tiles, rec, observed, out):
    span, ny, nz = out.shape[1:]
    count = rec.shape[1]
    nx = rows * tiles
    first = lax.axis_index("tile") * rows - ext
    cells = rec[...]
    plane = ny * nz
    x = cells // plane - first
    x = jnp.where(x < 0, x + nx, x)
    x = jnp.where(x >= nx, x - nx, x)
    line = x * ny + (cells // nz) % ny
    depth = cells % nz
    hit = (lax.broadcasted_iota(jnp.int32, (span * ny, count), 0) == line).astype(jnp.float32)
    column = lax.broadcasted_iota(jnp.int32, (nz, count), 0) == depth
    for k in range(steps + 1):
        value = observed[0, pl.ds(k - 1, 1), :] if k else jnp.ones((1, count), jnp.float32)
        weights = jnp.where(column, value, 0.0)
        dense = lax.dot_general(
            hit,
            weights,
            (((1,), (1,)), ((), ())),
            precision=lax.Precision.HIGHEST,
            preferred_element_type=jnp.float32,
        )
        out[k] = dense.reshape(span, ny, nz)


def sin_cos(t):
    u = t * t
    s = 1.0 / 6227020800.0
    for c in (-1.0 / 39916800.0, 1.0 / 362880.0, -1.0 / 5040.0, 1.0 / 120.0, -1.0 / 6.0, 1.0):
        s = s * u + c
    s = s * t
    c = 1.0 / 479001600.0
    for d in (-1.0 / 3628800.0, 1.0 / 40320.0, -1.0 / 720.0, 1.0 / 24.0, -0.5, 1.0):
        c = c * u + d
    return s, c


def coefficients_kernel(ext, coded, n_model, offset_ref, *refs):
    model_refs, (vsq, ge, gd, s2, sc, va_own) = refs[:n_model], refs[n_model:n_model + 6]
    model, sem = refs[n_model + 6:]
    rows, ny, nz = va_own.shape
    total = rows + 2 * ext
    copies = []
    if coded:
        j = lax.axis_index("shot")
        for index, ref in enumerate(model_refs):
            if index < 4:
                target = model.at[index, 0]
            else:
                target = model.at[j ^ ((index - 4) % 4), (index - 4) // 4 + 1]
            copies.append(pltpu.make_async_copy(ref, target, sem))
    else:
        for rel, ref in enumerate(model_refs):
            for field in range(4):
                copies.append(pltpu.make_async_copy(ref.at[field], model.at[field, rel], sem))
    for copy in copies:
        copy.start()
    for copy in copies:
        copy.wait()
    offset = offset_ref[0]
    around = rows * 4

    def model_row(n, i):
        at = lax.rem(i - ext + offset + around, around)
        return model[n, lax.div(at, rows), lax.rem(at, rows)].astype(jnp.float32).reshape(ny, nz)

    @pl.loop(1, total - 1, unroll=UNROLL)
    def _(i):
        va, eps, dlt, angle = (model_row(n, i) for n in range(4))
        sine, cosine = sin_cos(angle)
        vsq[i] = va * va
        ge[i] = 1.0 + 2.0 * eps
        gd[i] = 1.0 + 2.0 * dlt
        s2[i] = sine * sine
        sc[i] = 0.5 * sine * cosine

    @pl.loop(0, rows, unroll=UNROLL)
    def _(i):
        va_own[i] = model_row(0, i + ext)


class Stencils:
    def __init__(self, ny, nz, sums, slopes):
        self.nz, self.sums, self.slopes = nz, sums, slopes
        self.inner = slice(PAD, PAD + ny)
        self.up_one = slice(PAD - 1, PAD + ny - 1)
        self.down_one = slice(PAD + 1, PAD + ny + 1)
        lane = lax.broadcasted_iota(jnp.int32, (ny, nz), 1)
        self.not_first, self.not_last = lane > 0, lane < nz - 1

    def sum_and_slope(self, row):
        lines = row.shape[0]
        above = jnp.where(self.not_last[:lines], pltpu.roll(row, self.nz - 1, 1), 0.0)
        below = jnp.where(self.not_first[:lines], pltpu.roll(row, 1, 1), 0.0)
        return above + below, above - below

    def store_depth(self, turn, field, where, row):
        self.sums[turn][field][where], self.slopes[turn][field][where] = self.sum_and_slope(row)

    def crossed(self, turn, field, i):
        return self.slopes[turn][field][i + 1] - self.slopes[turn][field][i - 1]

    def flat(self, turn, ref, i, a2, c2, ab):
        side = ref[i - 1, self.inner] + ref[i + 1, self.inner]
        beside = ref[i, self.up_one] + ref[i, self.down_one]
        depth = a2 * self.sums[turn][0][i] - ab * self.crossed(turn, 0, i)
        return (c2 * side + beside - 4.0 * ref[i, self.inner]) + depth

    def steep(self, turn, ref, i, a2, c2, ab):
        side = ref[i - 1] + ref[i + 1]
        return (a2 * side - 2.0 * ref[i]) + (c2 * self.sums[turn][1][i] + ab * self.crossed(turn, 1, i))


def clear_edges(refs, total, ny):
    edge = jnp.zeros((PAD, refs[0].shape[2]), jnp.float32)

    @pl.loop(0, total, unroll=2)
    def _(i):
        for ref in refs:
            ref[i, 0:PAD] = edge
            ref[i, PAD + ny:] = edge


def forward_kernel(steps, ext, tiles, source_ref, wavelet_ref, vsq, ge, gd, s2, sc, dense, fwd, f_lo, f_hi, *refs):
    it = iter(refs)
    kept_h, kept_v, resid = next(it), next(it), next(it)
    press, shear = ([next(it) for _ in range(steps + 1)] for _ in range(2))
    sums, slopes = ([[next(it) for _ in range(2)] for _ in range(2)] for _ in range(2))
    code, sem, sem_code = it
    rows, ny, nz = fwd.shape[2:]
    total = rows + 2 * ext
    near = steps - 1
    copies = [
        pltpu.make_async_copy(fwd.at[0, 0], press[0].at[pl.ds(ext, rows), pl.ds(PAD, ny)], sem),
        pltpu.make_async_copy(fwd.at[0, 1], shear[0].at[pl.ds(ext, rows)], sem),
    ]
    code_copies = [
        pltpu.make_async_copy(f_lo, code.at[0], sem_code),
        pltpu.make_async_copy(f_hi, code.at[1], sem_code),
    ]
    for copy in code_copies + copies:
        copy.start()
    clear_edges(press[:steps], total, ny)
    ops = Stencils(ny, nz, sums, slopes)
    inner = ops.inner
    for copy in code_copies:
        copy.wait()

    @pl.loop(0, ext)
    def _(i):
        for side, base in ((0, 0), (1, ext + rows)):
            p = decoded(code[side, 0, i], STATE_BOUND).reshape(ny, nz)
            q = decoded(code[side, 1, i], STATE_BOUND).reshape(ny, nz)
            press[0][base + i, inner] = p
            shear[0][base + i] = q
            ops.store_depth(0, 0, base + i, p)
            ops.store_depth(0, 1, base + i, q)

    for copy in copies:
        copy.wait()

    @pl.loop(ext, ext + rows, unroll=2)
    def _(i):
        ops.store_depth(0, 0, i, press[0][i, inner])
        ops.store_depth(0, 1, i, shear[0][i])

    tile_first = lax.axis_index("tile") * rows
    nx = rows * tiles
    cell = source_ref[0]
    src_row = lax.rem(lax.div(cell, ny * nz) - tile_first + ext + nx, nx)
    src_y = lax.rem(lax.div(cell, nz), ny)
    src_here = lax.broadcasted_iota(jnp.int32, (1, nz), 1) == lax.rem(cell, nz)

    for k in range(steps):
        turn, last = k % 2, k == steps - 1
        p_new, q_new = press[k + 1], shear[k + 1]

        def one_row(i, keep):
            a2, ab = s2[i], sc[i]
            c2 = 1.0 - a2
            hp = ops.flat(turn, press[k], i, a2, c2, ab)
            hq = ops.steep(turn, shear[k], i, a2, c2, ab)
            if keep:
                kept_h[k, i - ext] = hp
                kept_v[k, i - ext] = hq
            p, q = press[k][i, inner], shear[k][i]
            speed = vsq[i]
            p_base = 2.0 * p - press[k - 1][i, inner] if k else p
            q_base = 2.0 * q - shear[k - 1][i] if k else q
            p = p_base + speed * (ge[i] * hp + hq)
            q = q_base + speed * (gd[i] * hp + hq)
            p_new[i, inner] = p
            q_new[i] = q
            if not last:
                ops.store_depth(1 - turn, 0, i, p)
                ops.store_depth(1 - turn, 1, i, q)

        @pl.loop(1 + k, ext, unroll=2)
        def _(i):
            one_row(i, False)
            one_row(total - 1 - i, False)

        pl.loop(ext, ext + rows, unroll=UNROLL)(lambda i: one_row(i, True))

        @pl.when((src_row >= 1 + k) & (src_row < total - 1 - k))
        def _():
            amount = jnp.where(src_here, wavelet_ref[0, k], 0.0)
            line = pl.ds(src_y, 1)
            p = p_new[src_row, pl.ds(PAD + src_y, 1)] + amount
            q = q_new[src_row, line] + amount
            p_new[src_row, pl.ds(PAD + src_y, 1)] = p
            q_new[src_row, line] = q
            if not last:
                for field, row in enumerate((p, q)):
                    total_row, slope_row = ops.sum_and_slope(row)
                    sums[1 - turn][field][src_row, line] = total_row
                    slopes[1 - turn][field][src_row, line] = slope_row

        @pl.loop(near - k, near + rows + k, unroll=2)
        def _(r):
            resid[k, r] = dense[0, r] * p_new[r + ext - near, inner] - dense[k + 1, r]


def adjoint_kernel(steps, ext, coded, offset_ref, vsq, ge, gd, s2, sc, va, kept_h, kept_v, resid, adj, a_lo, a_hi, *refs):
    it = iter(refs)
    outs = [next(it) for _ in range(4 if coded else 1)]
    lam, mu = ([next(it) for _ in range(steps + 1)] for _ in range(2))
    sums, slopes = ([[next(it) for _ in range(2)]] for _ in range(2))
    w1, w2, grads, code, sem, sem_code = it
    rows, ny, nz = adj.shape[2:]
    low_c = ext - steps
    total = rows + 2 * steps
    copies = [
        pltpu.make_async_copy(adj.at[0, 0], lam[0].at[pl.ds(steps, rows)], sem),
        pltpu.make_async_copy(adj.at[0, 1], mu[0].at[pl.ds(steps, rows)], sem),
    ]
    code_copies = [
        pltpu.make_async_copy(a_lo, code.at[0], sem_code),
        pltpu.make_async_copy(a_hi, code.at[1], sem_code),
    ]
    for copy in code_copies + copies:
        copy.start()
    clear_edges([w1], total, ny)
    ops = Stencils(ny, nz, sums, slopes)
    inner = ops.inner
    for copy in code_copies:
        copy.wait()

    @pl.loop(0, steps, unroll=2)
    def _(i):
        for side, base in ((0, 0), (1, steps + rows)):
            lam[0][base + i] = decoded(code[side, 0, i], STATE_BOUND).reshape(ny, nz)
            mu[0][base + i] = decoded(code[side, 1, i], STATE_BOUND).reshape(ny, nz)

    for copy in copies:
        copy.wait()

    for a in range(steps):
        k = steps - 1 - a

        @pl.loop(a, total - a, unroll=UNROLL)
        def _(i):
            l, m = lam[a][i], mu[a][i]
            c = i + low_c
            speed = vsq[c]
            first = speed * (ge[c] * l + gd[c] * m)
            second = speed * (l + m)
            w1[i, inner] = first
            w2[i] = second
            ops.store_depth(0, 0, i, first)
            ops.store_depth(0, 1, i, second)

        @pl.loop(a + 1, total - a - 1, unroll=UNROLL)
        def _(i):
            c = i + low_c
            a2, ab = s2[c], sc[c]
            c2 = 1.0 - a2
            h = ops.flat(0, w1, i, a2, c2, ab)
            v = ops.steep(0, w2, i, a2, c2, ab)
            l, m = lam[a][i], mu[a][i]
            l_base = 2.0 * l - lam[a - 1][i] if a else l
            m_base = 2.0 * m - mu[a - 1][i] if a else m
            lam[a + 1][i] = l_base + h + resid[k, i - 1]
            mu[a + 1][i] = m_base + v

    @pl.loop(0, rows, unroll=UNROLL)
    def _(r):
        sum_e = sum_d = sum_v = 0.0
        for k in range(steps):
            l, m = lam[steps - k][r + steps], mu[steps - k][r + steps]
            hp, hq = kept_h[k, r], kept_v[k, r]
            sum_e = sum_e + l * hp
            sum_d = sum_d + m * hp
            sum_v = sum_v + (l + m) * hq
        c = r + ext
        twice, twice_sq = 2.0 * va[r], 2.0 * vsq[c]
        grads[0, r] = twice * (ge[c] * sum_e + gd[c] * sum_d + sum_v)
        grads[1, r] = twice_sq * sum_e
        grads[2, r] = twice_sq * sum_d

    if not coded:
        outs[0][...] = grads[...]
        return
    quarter = ny // 4
    j = lax.axis_index("shot")
    powers = [power_of([grads[n]]) for n in range(3)]
    head = head_row(powers, quarter, offset_ref[0])
    for mask in range(4):
        y0 = pl.multiple_of((j ^ mask) * quarter, quarter)
        for n in range(3):
            part = grads[n, :, pl.ds(y0, quarter)]
            if mask:
                outs[mask][n * rows:(n + 1) * rows] = encoded(part, jnp.exp2(-powers[n]))
            else:
                outs[0][n * rows:(n + 1) * rows] = part
        if mask:
            outs[mask][3 * rows] = head


def gather_kernel(rows, offset_ref, own, *refs):
    codes, (here, *outs), acc = refs[:3], refs[3:7], refs[7]
    around = 4 * rows
    quarter, nz = own.shape[1:]
    zero = jnp.zeros((quarter, nz), jnp.float32)

    @pl.loop(0, around, unroll=8)
    def _(x):
        for n in range(3):
            acc[n, x] = zero

    offset = offset_ref[0]

    for r in range(rows):
        for n in range(3):
            acc[n, lax.rem(r + offset, around)] = own[n * rows + r]

    for code in codes:
        head = code[3 * rows].astype(jnp.int32).astype(jnp.float32)
        theirs = jnp.max(head[8:9]).astype(jnp.int32)
        scales = scales_of(head)
        for n in range(3):
            part = decoded(code[n * rows:(n + 1) * rows], scales[n])
            for r in range(rows):
                acc[n, lax.rem(r + theirs, around)] += part[r]

    here[...] = acc[:, 0:rows].reshape(here.shape)
    for rel in range(1, 4):
        parts = [acc[n, rel * rows:(rel + 1) * rows] for n in range(3)]
        powers = [power_of([part]) for part in parts]
        for n in range(3):
            outs[rel - 1][n * rows:(n + 1) * rows] = encoded(parts[n], jnp.exp2(-powers[n]))
        outs[rel - 1][3 * rows] = head_row(powers, quarter, 0)


def finish_kernel(rows, own, *refs):
    codes, outs = refs[:3], refs[3:]
    scales = [scales_of(code[3 * rows].astype(jnp.int32).astype(jnp.float32)) for code in codes]
    for n in range(3):
        total = own[n * rows:(n + 1) * rows]
        for code, scale in zip(codes, scales):
            total = total + decoded(code[n * rows:(n + 1) * rows], scale[n])
        outs[n][...] = total


def on_device(
    velocity,
    epsilon,
    delta,
    tilt,
    forward_state,
    adjoint_state,
    offsets,
    src_cells,
    rec_cells,
    wavelet,
    observed,
):
    rows, ny, nz = velocity.shape
    tiles = lax.axis_size("tile")
    shots = lax.axis_size("shot")
    steps = wavelet.shape[1]
    ext = 2 * steps - 1
    near = steps - 1
    total = rows + 2 * ext
    span = rows + 2 * near
    assert rows >= ext
    coded = tiles == 4 and shots == 4
    f32, i16 = jnp.float32, jnp.int16

    small = pltpu.CompilerParams(vmem_limit_bytes=4 * 1024 * 1024)

    def struct(*shape, dtype=f32):
        return jax.ShapeDtypeStruct(shape, dtype)

    def edge_codes(state, width):
        return pl.pallas_call(
            functools.partial(edges_kernel, width),
            out_shape=[struct(2, width, ny, nz, dtype=i16)] * 2,
            in_specs=vmem(1),
            out_specs=vmem(2),
            compiler_params=small,
            name="edges",
        )(state)

    def to_neighbours(up, down):
        return passed_along(up, "tile", 1), passed_along(down, "tile", -1)

    f_codes = edge_codes(forward_state, ext)
    a_codes = edge_codes(adjoint_state, steps)
    dense = pl.pallas_call(
        functools.partial(receivers_kernel, steps, near, rows, tiles),
        out_shape=struct(steps + 1, span, ny, nz),
        in_specs=vmem(2),
        out_specs=pl.BlockSpec(memory_space=pltpu.VMEM),
        compiler_params=pltpu.CompilerParams(vmem_limit_bytes=16 * 1024 * 1024),
        name="receivers",
    )(rec_cells, observed)

    if coded:
        j = lax.axis_index("shot")
        quarter_field = lax.select_n(j, velocity, epsilon, delta, tilt)
        ahead = passed_along(quarter_field, "tile", -1)
        behind = passed_along(quarter_field, "tile", 1)
        across = passed_along(quarter_field, "tile", 2)
        f_lo, f_hi = to_neighbours(*f_codes)
        ahead, behind, a_codes, dense = lax.optimization_barrier((ahead, behind, a_codes, dense))
        beyond = [swapped(piece, 2) for piece in (ahead, behind)]
        a_codes, beyond = lax.optimization_barrier((a_codes, beyond))
        a_lo, a_hi = to_neighbours(*a_codes)
        model_refs = [velocity, epsilon, delta, tilt]
        for piece, other in ((ahead, beyond[0]), (across, swapped(across, 2)), (behind, beyond[1])):
            model_refs += [piece, swapped(piece, 1), other, swapped(other, 1)]
        shift = offsets
    else:
        nbits = max(1, (tiles - 1).bit_length())
        block = jnp.stack([velocity, epsilon, delta, tilt])
        whole = offsets[0] // rows
        for bit in range(nbits):
            moved = passed_along(block, "tile", -(1 << bit))
            block = jnp.where(jnp.bitwise_and(jnp.right_shift(whole, bit), 1) == 1, moved, block)
        model_refs = [block] + [passed_along(block, "tile", -by) for by in (1, 2, -1)]
        f_lo, f_hi = to_neighbours(*f_codes)
        a_lo, a_hi = to_neighbours(*a_codes)
        shift = offsets % rows

    field = (total, ny, nz)
    *coefficients, va = pl.pallas_call(
        functools.partial(coefficients_kernel, ext, coded, len(model_refs)),
        out_shape=[struct(*field)] * 5 + [struct(rows, ny, nz)],
        in_specs=smem(1) + anywhere(len(model_refs)),
        out_specs=vmem(6),
        scratch_shapes=[
            pltpu.VMEM((4, 4, rows, ny // 8, 8, nz), jnp.bfloat16),
            pltpu.SemaphoreType.DMA,
        ],
        compiler_params=pltpu.CompilerParams(vmem_limit_bytes=16 * 1024 * 1024),
        name="coefficients",
    )(shift, *map(tiled, model_refs))

    kept_h, kept_v, resid = pl.pallas_call(
        functools.partial(forward_kernel, steps, ext, tiles),
        out_shape=[struct(steps, rows, ny, nz)] * 2 + [struct(steps, span, ny, nz)],
        in_specs=smem(2) + vmem(6) + anywhere(3),
        out_specs=vmem(3),
        scratch_shapes=[
            *[pltpu.VMEM((total, ny + 2 * PAD, nz), f32)] * (steps + 1),
            *[pltpu.VMEM(field, f32)] * (steps + 1 + 8),
            pltpu.VMEM((2, 2, ext, ny // 8, 8, nz), i16),
            *[pltpu.SemaphoreType.DMA] * 2,
        ],
        compiler_params=pltpu.CompilerParams(vmem_limit_bytes=32 * 1024 * 1024),
        name="forward",
    )(src_cells, wavelet, *coefficients, dense, forward_state, *map(tiled, (f_lo, f_hi)))

    quarter = ny // 4
    if coded:
        wave_outs = [struct(3 * rows, quarter, nz)] + [struct(3 * rows + 1, quarter, nz, dtype=i16)] * 3
    else:
        wave_outs = [struct(3, rows, ny, nz)]
    narrow = (rows + 2 * steps, ny, nz)
    waves = pl.pallas_call(
        functools.partial(adjoint_kernel, steps, ext, coded),
        out_shape=wave_outs,
        in_specs=smem(1) + vmem(9) + anywhere(3),
        out_specs=vmem(len(wave_outs)),
        scratch_shapes=[
            *[pltpu.VMEM(narrow, f32)] * (2 * (steps + 1) + 4),
            pltpu.VMEM((rows + 2 * steps, ny + 2 * PAD, nz), f32),
            pltpu.VMEM(narrow, f32),
            pltpu.VMEM((3, rows, ny, nz), f32),
            pltpu.VMEM((2, 2, steps, ny // 8, 8, nz), i16),
            *[pltpu.SemaphoreType.DMA] * 2,
        ],
        compiler_params=pltpu.CompilerParams(vmem_limit_bytes=24 * 1024 * 1024),
        name="adjoint",
    )(offsets, *coefficients, va, kept_h, kept_v, resid, adjoint_state, *map(tiled, (a_lo, a_hi)))

    if not coded:
        (gradients,) = waves
        within = shift[0]
        spread = jnp.zeros((3, 2 * rows, ny, nz), f32)
        spread = lax.dynamic_update_slice_in_dim(spread, gradients, within, 1)
        combined = spread[:, :rows] + passed_along(spread[:, rows:], "tile", 1)
        for bit in range(nbits):
            moved = passed_along(combined, "tile", 1 << bit)
            combined = jnp.where(jnp.bitwise_and(jnp.right_shift(whole, bit), 1) == 1, moved, combined)
        summed = lax.psum(combined, "shot")
        share = ny // shots
        result = lax.dynamic_slice_in_dim(summed, lax.axis_index("shot") * share, share, 2)
        return (result[0], result[1], result[2])

    own, *sent = waves
    received = [swapped(code, mask) for mask, code in zip((1, 2, 3), sent)]
    part = struct(3 * rows + 1, quarter, nz, dtype=i16)
    here, *parts = pl.pallas_call(
        functools.partial(gather_kernel, rows),
        out_shape=[jax.ShapeDtypeStruct((3 * rows, quarter, nz), f32), part, part, part],
        in_specs=smem(1) + vmem(4),
        out_specs=vmem(4),
        scratch_shapes=[pltpu.VMEM((3, 4 * rows, quarter, nz), f32)],
        compiler_params=small,
        name="gather",
    )(offsets, own, *received)
    arrived = [passed_along(p, "tile", rel) for rel, p in zip((1, 2, 3), parts)]
    return tuple(
        pl.pallas_call(
            functools.partial(finish_kernel, rows),
            out_shape=[jax.ShapeDtypeStruct((rows, quarter, nz), f32)] * 3,
            in_specs=vmem(4),
            out_specs=vmem(3),
            compiler_params=small,
            name="finish",
        )(here, *arrived)
    )


def solution(mesh):
    placed = (
        P(("groups", "tile"), None, None),
        P(("groups", "tile"), None, None),
        P(("groups", "tile"), None, None),
        P(("groups", "tile"), None, None),
        P(("groups", "shot"), None, "tile", None, None),
        P(("groups", "shot"), None, "tile", None, None),
        P(("groups", "shot")),
        P(("groups", "shot")),
        P(("groups", "shot"), None),
        P(("groups", "shot"), None),
        P(("groups", "shot"), None, None),
    )
    return jax.shard_map(
        on_device,
        mesh=mesh,
        in_specs=placed,
        out_specs=(
            P(("groups", "tile"), "shot", None),
            P(("groups", "tile"), "shot", None),
            P(("groups", "tile"), "shot", None),
        ),
        check_vma=False,
    )
```

```python
import functools

import jax
import jax.numpy as jnp
from jax import lax
from jax.experimental import pallas as pl
from jax.experimental.pallas import tpu as pltpu
from jax.sharding import PartitionSpec as P

TOP = 32767.0
PAD = 8
UNROLL = 4
SHORT = pl.CostEstimate(flops=0, bytes_accessed=1024, transcendentals=0)
EARLY = pl.CostEstimate(flops=0, bytes_accessed=16 * 1024 * 1024, transcendentals=0)
STATE_BOUND = 2.0


def passed_along(x, axis, by):
    count = lax.axis_size(axis)
    return lax.ppermute(x, axis, [(i, (i + by) % count) for i in range(count)])


def swapped(x, mask):
    count = lax.axis_size("shot")
    return lax.ppermute(x, "shot", [(i, i ^ mask) for i in range(count)])


def encoded(x, inverse):
    root = jnp.sqrt(jnp.sqrt(jnp.abs(x) * inverse))
    level = jnp.minimum(root * TOP + 0.5, TOP)
    return jnp.where(x < 0, -level, level).astype(jnp.int32).astype(jnp.int16)


def decoded(code, scale):
    level = code.astype(jnp.int32).astype(jnp.float32) * (1.0 / TOP)
    square = level * level
    value = square * square * scale
    return jnp.where(level < 0, -value, value)


def power_of(blocks):
    top = functools.reduce(jnp.maximum, [jnp.max(jnp.abs(x), axis=0) for x in blocks])
    top = jnp.max(jnp.max(top, axis=0, keepdims=True), axis=1, keepdims=True)
    return jnp.ceil(jnp.log2(jnp.maximum(top, 1e-30))) + 1.0


def head_row(powers, lines, offset):
    line = lax.broadcasted_iota(jnp.int32, (lines, 128), 0)
    head = jnp.full((lines, 128), offset, jnp.int32)
    for n, power in enumerate(powers):
        head = jnp.where(line == n, jnp.broadcast_to(power, (lines, 128)).astype(jnp.int32), head)
    return head.astype(jnp.int16)


def scales_of(head):
    return [jnp.exp2(head[n:n + 1]) for n in range(3)]


def tiled(x):
    return x.reshape(x.shape[:-2] + (x.shape[-2] // 8, 8, x.shape[-1]))


def vmem(count):
    return [pl.BlockSpec(memory_space=pltpu.VMEM)] * count


def smem(count):
    return [pl.BlockSpec(memory_space=pltpu.SMEM)] * count


def anywhere(count):
    return [pl.BlockSpec(memory_space=pl.ANY)] * count


def edges_kernel(widths, fwd, adj, up, down):
    rows = fwd.shape[2]
    n = 0
    for state, width in zip((fwd, adj), widths):
        for field in range(2):
            for i in range(width):
                up[n] = encoded(state[0, field, rows - width + i], 1.0 / STATE_BOUND)
                down[n] = encoded(state[0, field, i], 1.0 / STATE_BOUND)
                n += 1


def receivers_kernel(steps, ext, rows, tiles, rec, observed, out):
    span, ny, nz = out.shape[1:]
    count = rec.shape[1]
    nx = rows * tiles
    first = lax.axis_index("tile") * rows - ext
    cells = rec[...]
    plane = ny * nz
    x = cells // plane - first
    x = jnp.where(x < 0, x + nx, x)
    x = jnp.where(x >= nx, x - nx, x)
    line = x * ny + (cells // nz) % ny
    depth = cells % nz
    hit = lax.broadcasted_iota(jnp.int32, (span * ny, count), 0) == line
    hit = jnp.where(hit, 1.0, 0.0).astype(jnp.bfloat16)
    column = lax.broadcasted_iota(jnp.int32, (nz, count), 0) == depth

    def dense(weights):
        dims = (((1,), (1,)), ((), ()))
        return lax.dot_general(hit, weights, dims, preferred_element_type=jnp.float32).reshape(span, ny, nz)

    out[0] = dense(jnp.where(column, 1.0, 0.0).astype(jnp.bfloat16))
    for k in range(steps):
        rest = jnp.where(column, observed[0, k:k + 1, :], 0.0)
        total = None
        for _ in range(3):
            term = rest.astype(jnp.bfloat16)
            rest = rest - term.astype(jnp.float32)
            total = dense(term) if total is None else total + dense(term)
        out[k + 1] = total


def sin_cos(t):
    u = t * t
    s = 1.0 / 6227020800.0
    for c in (-1.0 / 39916800.0, 1.0 / 362880.0, -1.0 / 5040.0, 1.0 / 120.0, -1.0 / 6.0, 1.0):
        s = s * u + c
    s = s * t
    c = 1.0 / 479001600.0
    for d in (-1.0 / 3628800.0, 1.0 / 40320.0, -1.0 / 720.0, 1.0 / 24.0, -0.5, 1.0):
        c = c * u + d
    return s, c


def coefficients_kernel(ext, coded, n_model, offset_ref, *refs):
    model_refs, (vsq, ge, gd, s2, sc, va_own) = refs[:n_model], refs[n_model:n_model + 6]
    model, sem = refs[n_model + 6:]
    rows, ny, nz = va_own.shape
    total = rows + 2 * ext
    copies = []
    if coded:
        j = lax.axis_index("shot")
        for index, ref in enumerate(model_refs):
            if index < 4:
                target = model.at[index, 0]
            else:
                target = model.at[j ^ ((index - 4) % 4), (index - 4) // 4 + 1]
            copies.append(pltpu.make_async_copy(ref, target, sem))
    else:
        for rel, ref in enumerate(model_refs):
            for field in range(4):
                copies.append(pltpu.make_async_copy(ref.at[field], model.at[field, rel], sem))
    for copy in copies:
        copy.start()
    for copy in copies:
        copy.wait()
    offset = offset_ref[0]
    around = rows * 4

    def model_row(n, i):
        at = lax.rem(i - ext + offset + around, around)
        return model[n, lax.div(at, rows), lax.rem(at, rows)].astype(jnp.float32).reshape(ny, nz)

    @pl.loop(1, total - 1, unroll=UNROLL)
    def _(i):
        va, eps, dlt, angle = (model_row(n, i) for n in range(4))
        sine, cosine = sin_cos(angle)
        vsq[i] = va * va
        ge[i] = 1.0 + 2.0 * eps
        gd[i] = 1.0 + 2.0 * dlt
        s2[i] = sine * sine
        sc[i] = 0.5 * sine * cosine

    @pl.loop(0, rows, unroll=UNROLL)
    def _(i):
        va_own[i] = model_row(0, i + ext)


class Stencils:
    def __init__(self, ny, nz, sums, slopes):
        self.nz, self.sums, self.slopes = nz, sums, slopes
        self.inner = slice(PAD, PAD + ny)
        self.up_one = slice(PAD - 1, PAD + ny - 1)
        self.down_one = slice(PAD + 1, PAD + ny + 1)
        lane = lax.broadcasted_iota(jnp.int32, (ny, nz), 1)
        self.not_first, self.not_last = lane > 0, lane < nz - 1

    def sum_and_slope(self, row):
        lines = row.shape[0]
        above = jnp.where(self.not_last[:lines], pltpu.roll(row, self.nz - 1, 1), 0.0)
        below = jnp.where(self.not_first[:lines], pltpu.roll(row, 1, 1), 0.0)
        return above + below, above - below

    def store_depth(self, turn, field, where, row):
        self.sums[turn][field][where], self.slopes[turn][field][where] = self.sum_and_slope(row)

    def crossed(self, turn, field, i):
        return self.slopes[turn][field][i + 1] - self.slopes[turn][field][i - 1]

    def flat(self, turn, ref, i, a2, c2, ab):
        side = ref[i - 1, self.inner] + ref[i + 1, self.inner]
        beside = ref[i, self.up_one] + ref[i, self.down_one]
        depth = a2 * self.sums[turn][0][i] - ab * self.crossed(turn, 0, i)
        return (c2 * side + beside - 4.0 * ref[i, self.inner]) + depth

    def steep(self, turn, ref, i, a2, c2, ab):
        side = ref[i - 1] + ref[i + 1]
        return (a2 * side - 2.0 * ref[i]) + (c2 * self.sums[turn][1][i] + ab * self.crossed(turn, 1, i))


def clear_edges(refs, total, ny):
    edge = jnp.zeros((PAD, refs[0].shape[2]), jnp.float32)

    @pl.loop(0, total, unroll=2)
    def _(i):
        for ref in refs:
            ref[i, 0:PAD] = edge
            ref[i, PAD + ny:] = edge


def forward_kernel(steps, ext, tiles, source_ref, wavelet_ref, vsq, ge, gd, s2, sc, dense, fwd, f_lo, f_hi, *refs):
    it = iter(refs)
    kept_h, kept_v, resid = next(it), next(it), next(it)
    press, shear = ([next(it) for _ in range(steps + 1)] for _ in range(2))
    sums, slopes = ([[next(it) for _ in range(2)] for _ in range(2)] for _ in range(2))
    code, sem, sem_code = it
    rows, ny, nz = fwd.shape[2:]
    total = rows + 2 * ext
    near = steps - 1
    copies = [
        pltpu.make_async_copy(fwd.at[0, 0], press[0].at[pl.ds(ext, rows), pl.ds(PAD, ny)], sem),
        pltpu.make_async_copy(fwd.at[0, 1], shear[0].at[pl.ds(ext, rows)], sem),
    ]
    code_copies = [
        pltpu.make_async_copy(f_lo.at[pl.ds(0, 2 * ext)], code.at[0], sem_code),
        pltpu.make_async_copy(f_hi.at[pl.ds(0, 2 * ext)], code.at[1], sem_code),
    ]
    for copy in code_copies + copies:
        copy.start()
    clear_edges(press[:steps], total, ny)
    ops = Stencils(ny, nz, sums, slopes)
    inner = ops.inner
    for copy in code_copies:
        copy.wait()

    @pl.loop(0, ext)
    def _(i):
        for side, base in ((0, 0), (1, ext + rows)):
            p = decoded(code[side, i], STATE_BOUND).reshape(ny, nz)
            q = decoded(code[side, ext + i], STATE_BOUND).reshape(ny, nz)
            press[0][base + i, inner] = p
            shear[0][base + i] = q
            ops.store_depth(0, 0, base + i, p)
            ops.store_depth(0, 1, base + i, q)

    for copy in copies:
        copy.wait()

    @pl.loop(ext, ext + rows, unroll=2)
    def _(i):
        ops.store_depth(0, 0, i, press[0][i, inner])
        ops.store_depth(0, 1, i, shear[0][i])

    tile_first = lax.axis_index("tile") * rows
    nx = rows * tiles
    cell = source_ref[0]
    src_row = lax.rem(lax.div(cell, ny * nz) - tile_first + ext + nx, nx)
    src_y = lax.rem(lax.div(cell, nz), ny)
    src_here = lax.broadcasted_iota(jnp.int32, (1, nz), 1) == lax.rem(cell, nz)

    for k in range(steps):
        turn, last = k % 2, k == steps - 1
        p_new, q_new = press[k + 1], shear[k + 1]

        def one_row(i, keep):
            a2, ab = s2[i], sc[i]
            c2 = 1.0 - a2
            hp = ops.flat(turn, press[k], i, a2, c2, ab)
            hq = ops.steep(turn, shear[k], i, a2, c2, ab)
            if keep:
                kept_h[k, i - ext] = hp
                kept_v[k, i - ext] = hq
            p, q = press[k][i, inner], shear[k][i]
            speed = vsq[i]
            p_base = 2.0 * p - press[k - 1][i, inner] if k else p
            q_base = 2.0 * q - shear[k - 1][i] if k else q
            p = p_base + speed * (ge[i] * hp + hq)
            q = q_base + speed * (gd[i] * hp + hq)
            p_new[i, inner] = p
            q_new[i] = q
            if not last:
                ops.store_depth(1 - turn, 0, i, p)
                ops.store_depth(1 - turn, 1, i, q)

        @pl.loop(1 + k, ext, unroll=2)
        def _(i):
            one_row(i, False)
            one_row(total - 1 - i, False)

        pl.loop(ext, ext + rows, unroll=UNROLL)(lambda i: one_row(i, True))

        @pl.when((src_row >= 1 + k) & (src_row < total - 1 - k))
        def _():
            amount = jnp.where(src_here, wavelet_ref[0, k], 0.0)
            line = pl.ds(src_y, 1)
            p = p_new[src_row, pl.ds(PAD + src_y, 1)] + amount
            q = q_new[src_row, line] + amount
            p_new[src_row, pl.ds(PAD + src_y, 1)] = p
            q_new[src_row, line] = q
            if not last:
                for field, row in enumerate((p, q)):
                    total_row, slope_row = ops.sum_and_slope(row)
                    sums[1 - turn][field][src_row, line] = total_row
                    slopes[1 - turn][field][src_row, line] = slope_row

        @pl.loop(near - k, near + rows + k, unroll=2)
        def _(r):
            resid[k, r] = dense[0, r] * p_new[r + ext - near, inner] - dense[k + 1, r]


def adjoint_kernel(steps, ext, coded, offset_ref, vsq, ge, gd, s2, sc, va, kept_h, kept_v, resid, adj, a_lo, a_hi, *refs):
    it = iter(refs)
    outs = [next(it) for _ in range(4 if coded else 1)]
    lam, mu = ([next(it) for _ in range(steps + 1)] for _ in range(2))
    sums, slopes = ([[next(it) for _ in range(2)]] for _ in range(2))
    w1, w2, grads, code, sem, sem_code = it
    rows, ny, nz = adj.shape[2:]
    low_c = ext - steps
    total = rows + 2 * steps
    copies = [
        pltpu.make_async_copy(adj.at[0, 0], lam[0].at[pl.ds(steps, rows)], sem),
        pltpu.make_async_copy(adj.at[0, 1], mu[0].at[pl.ds(steps, rows)], sem),
    ]
    code_copies = [
        pltpu.make_async_copy(a_lo.at[pl.ds(2 * ext, 2 * steps)], code.at[0], sem_code),
        pltpu.make_async_copy(a_hi.at[pl.ds(2 * ext, 2 * steps)], code.at[1], sem_code),
    ]
    for copy in code_copies + copies:
        copy.start()
    clear_edges([w1], total, ny)
    ops = Stencils(ny, nz, sums, slopes)
    inner = ops.inner
    for copy in code_copies:
        copy.wait()

    @pl.loop(0, steps, unroll=2)
    def _(i):
        for side, base in ((0, 0), (1, steps + rows)):
            lam[0][base + i] = decoded(code[side, i], STATE_BOUND).reshape(ny, nz)
            mu[0][base + i] = decoded(code[side, steps + i], STATE_BOUND).reshape(ny, nz)

    for copy in copies:
        copy.wait()

    for a in range(steps):
        k = steps - 1 - a

        @pl.loop(a, total - a, unroll=UNROLL)
        def _(i):
            l, m = lam[a][i], mu[a][i]
            c = i + low_c
            speed = vsq[c]
            first = speed * (ge[c] * l + gd[c] * m)
            second = speed * (l + m)
            w1[i, inner] = first
            w2[i] = second
            ops.store_depth(0, 0, i, first)
            ops.store_depth(0, 1, i, second)

        @pl.loop(a + 1, total - a - 1, unroll=UNROLL)
        def _(i):
            c = i + low_c
            a2, ab = s2[c], sc[c]
            c2 = 1.0 - a2
            h = ops.flat(0, w1, i, a2, c2, ab)
            v = ops.steep(0, w2, i, a2, c2, ab)
            l, m = lam[a][i], mu[a][i]
            l_base = 2.0 * l - lam[a - 1][i] if a else l
            m_base = 2.0 * m - mu[a - 1][i] if a else m
            lam[a + 1][i] = l_base + h + resid[k, i - 1]
            mu[a + 1][i] = m_base + v

    @pl.loop(0, rows, unroll=UNROLL)
    def _(r):
        sum_e = sum_d = sum_v = 0.0
        for k in range(steps):
            l, m = lam[steps - k][r + steps], mu[steps - k][r + steps]
            hp, hq = kept_h[k, r], kept_v[k, r]
            sum_e = sum_e + l * hp
            sum_d = sum_d + m * hp
            sum_v = sum_v + (l + m) * hq
        c = r + ext
        twice, twice_sq = 2.0 * va[r], 2.0 * vsq[c]
        grads[0, r] = twice * (ge[c] * sum_e + gd[c] * sum_d + sum_v)
        grads[1, r] = twice_sq * sum_e
        grads[2, r] = twice_sq * sum_d

    if not coded:
        outs[0][...] = grads[...]
        return
    quarter = ny // 4
    j = lax.axis_index("shot")
    powers = [power_of([grads[n]]) for n in range(3)]
    head = head_row(powers, quarter, offset_ref[0])
    for mask in range(4):
        y0 = pl.multiple_of((j ^ mask) * quarter, quarter)
        for n in range(3):
            part = grads[n, :, pl.ds(y0, quarter)]
            if mask:
                outs[mask][n * rows:(n + 1) * rows] = encoded(part, jnp.exp2(-powers[n]))
            else:
                outs[0][n * rows:(n + 1) * rows] = part
        if mask:
            outs[mask][3 * rows] = head


def gather_kernel(rows, offset_ref, own, *refs):
    codes, (here, *outs), acc = refs[:3], refs[3:7], refs[7]
    around = 4 * rows
    quarter, nz = own.shape[1:]
    zero = jnp.zeros((quarter, nz), jnp.float32)

    @pl.loop(0, around, unroll=8)
    def _(x):
        for n in range(3):
            acc[n, x] = zero

    offset = offset_ref[0]

    for r in range(rows):
        for n in range(3):
            acc[n, lax.rem(r + offset, around)] = own[n * rows + r]

    for code in codes:
        head = code[3 * rows].astype(jnp.int32).astype(jnp.float32)
        theirs = jnp.max(head[8:9]).astype(jnp.int32)
        scales = scales_of(head)
        for n in range(3):
            part = decoded(code[n * rows:(n + 1) * rows], scales[n])
            for r in range(rows):
                acc[n, lax.rem(r + theirs, around)] += part[r]

    here[...] = acc[:, 0:rows].reshape(here.shape)
    for rel in range(1, 4):
        parts = [acc[n, rel * rows:(rel + 1) * rows] for n in range(3)]
        powers = [power_of([part]) for part in parts]
        for n in range(3):
            outs[rel - 1][n * rows:(n + 1) * rows] = encoded(parts[n], jnp.exp2(-powers[n]))
        outs[rel - 1][3 * rows] = head_row(powers, quarter, 0)


def finish_kernel(rows, own, *refs):
    codes, outs = refs[:3], refs[3:]
    scales = [scales_of(code[3 * rows].astype(jnp.int32).astype(jnp.float32)) for code in codes]
    for n in range(3):
        total = own[n * rows:(n + 1) * rows]
        for code, scale in zip(codes, scales):
            total = total + decoded(code[n * rows:(n + 1) * rows], scale[n])
        outs[n][...] = total


def on_device(
    velocity,
    epsilon,
    delta,
    tilt,
    forward_state,
    adjoint_state,
    offsets,
    src_cells,
    rec_cells,
    wavelet,
    observed,
):
    rows, ny, nz = velocity.shape
    tiles = lax.axis_size("tile")
    shots = lax.axis_size("shot")
    steps = wavelet.shape[1]
    ext = 2 * steps - 1
    near = steps - 1
    total = rows + 2 * ext
    span = rows + 2 * near
    assert rows >= ext
    coded = tiles == 4 and shots == 4
    f32, i16 = jnp.float32, jnp.int16

    small = pltpu.CompilerParams(vmem_limit_bytes=4 * 1024 * 1024)

    def struct(*shape, dtype=f32):
        return jax.ShapeDtypeStruct(shape, dtype)

    codes = pl.pallas_call(
        functools.partial(edges_kernel, (ext, steps)),
        out_shape=[struct(2 * (ext + steps), ny, nz, dtype=i16)] * 2,
        in_specs=vmem(2),
        out_specs=vmem(2),
        compiler_params=small,
        cost_estimate=EARLY,
        name="edges",
    )(forward_state, adjoint_state)

    dense = pl.pallas_call(
        functools.partial(receivers_kernel, steps, near, rows, tiles),
        out_shape=struct(steps + 1, span, ny, nz),
        in_specs=vmem(2),
        out_specs=pl.BlockSpec(memory_space=pltpu.VMEM),
        compiler_params=pltpu.CompilerParams(vmem_limit_bytes=8 * 1024 * 1024),
        cost_estimate=EARLY,
        name="receivers",
    )(rec_cells, observed)

    def to_neighbours(up, down):
        return passed_along(up, "tile", 1), passed_along(down, "tile", -1)

    if coded:
        share = lax.select_n(lax.axis_index("shot"), velocity, epsilon, delta, tilt)
        ahead = passed_along(share, "tile", -1)
        behind = passed_along(share, "tile", 1)
        ahead, behind, codes, dense = lax.optimization_barrier((ahead, behind, codes, dense))
        across = passed_along(ahead, "tile", -1)
        halo_lo, halo_hi = to_neighbours(*codes)
        far_ahead, far_behind, far_across = (swapped(piece, 2) for piece in (ahead, behind, across))
        model_refs = [velocity, epsilon, delta, tilt]
        for piece, other in ((ahead, far_ahead), (across, far_across), (behind, far_behind)):
            model_refs += [piece, swapped(piece, 1), other, swapped(other, 1)]
        shift = offsets
    else:
        nbits = max(1, (tiles - 1).bit_length())
        block = jnp.stack([velocity, epsilon, delta, tilt])
        whole = offsets[0] // rows
        for bit in range(nbits):
            moved = passed_along(block, "tile", -(1 << bit))
            block = jnp.where(jnp.bitwise_and(jnp.right_shift(whole, bit), 1) == 1, moved, block)
        model_refs = [block] + [passed_along(block, "tile", -by) for by in (1, 2, -1)]
        halo_lo, halo_hi = to_neighbours(*codes)
        shift = offsets % rows

    field = (total, ny, nz)
    *coefficients, va = pl.pallas_call(
        functools.partial(coefficients_kernel, ext, coded, len(model_refs)),
        out_shape=[struct(*field)] * 5 + [struct(rows, ny, nz)],
        in_specs=smem(1) + anywhere(len(model_refs)),
        out_specs=vmem(6),
        scratch_shapes=[
            pltpu.VMEM((4, 4, rows, ny // 8, 8, nz), jnp.bfloat16),
            pltpu.SemaphoreType.DMA,
        ],
        compiler_params=pltpu.CompilerParams(vmem_limit_bytes=16 * 1024 * 1024),
        cost_estimate=SHORT,
        name="coefficients",
    )(shift, *map(tiled, model_refs))

    kept_h, kept_v, resid = pl.pallas_call(
        functools.partial(forward_kernel, steps, ext, tiles),
        out_shape=[struct(steps, rows, ny, nz)] * 2 + [struct(steps, span, ny, nz)],
        in_specs=smem(2) + vmem(6) + anywhere(3),
        out_specs=vmem(3),
        scratch_shapes=[
            *[pltpu.VMEM((total, ny + 2 * PAD, nz), f32)] * (steps + 1),
            *[pltpu.VMEM(field, f32)] * (steps + 1 + 8),
            pltpu.VMEM((2, 2 * ext, ny // 8, 8, nz), i16),
            *[pltpu.SemaphoreType.DMA] * 2,
        ],
        compiler_params=pltpu.CompilerParams(vmem_limit_bytes=32 * 1024 * 1024),
        name="forward",
    )(src_cells, wavelet, *coefficients, dense, forward_state, *map(tiled, (halo_lo, halo_hi)))

    quarter = ny // 4
    if coded:
        wave_outs = [struct(3 * rows, quarter, nz)] + [struct(3 * rows + 1, quarter, nz, dtype=i16)] * 3
    else:
        wave_outs = [struct(3, rows, ny, nz)]
    narrow = (rows + 2 * steps, ny, nz)
    waves = pl.pallas_call(
        functools.partial(adjoint_kernel, steps, ext, coded),
        out_shape=wave_outs,
        in_specs=smem(1) + vmem(9) + anywhere(3),
        out_specs=vmem(len(wave_outs)),
        scratch_shapes=[
            *[pltpu.VMEM(narrow, f32)] * (2 * (steps + 1) + 4),
            pltpu.VMEM((rows + 2 * steps, ny + 2 * PAD, nz), f32),
            pltpu.VMEM(narrow, f32),
            pltpu.VMEM((3, rows, ny, nz), f32),
            pltpu.VMEM((2, 2 * steps, ny // 8, 8, nz), i16),
            *[pltpu.SemaphoreType.DMA] * 2,
        ],
        compiler_params=pltpu.CompilerParams(vmem_limit_bytes=24 * 1024 * 1024),
        name="adjoint",
    )(offsets, *coefficients, va, kept_h, kept_v, resid, adjoint_state, *map(tiled, (halo_lo, halo_hi)))

    if not coded:
        (gradients,) = waves
        within = shift[0]
        spread = jnp.zeros((3, 2 * rows, ny, nz), f32)
        spread = lax.dynamic_update_slice_in_dim(spread, gradients, within, 1)
        combined = spread[:, :rows] + passed_along(spread[:, rows:], "tile", 1)
        for bit in range(nbits):
            moved = passed_along(combined, "tile", 1 << bit)
            combined = jnp.where(jnp.bitwise_and(jnp.right_shift(whole, bit), 1) == 1, moved, combined)
        summed = lax.psum(combined, "shot")
        share = ny // shots
        result = lax.dynamic_slice_in_dim(summed, lax.axis_index("shot") * share, share, 2)
        return (result[0], result[1], result[2])

    own, *sent = waves
    received = [swapped(code, mask) for mask, code in zip((1, 2, 3), sent)]
    part = struct(3 * rows + 1, quarter, nz, dtype=i16)
    here, *parts = pl.pallas_call(
        functools.partial(gather_kernel, rows),
        out_shape=[jax.ShapeDtypeStruct((3 * rows, quarter, nz), f32), part, part, part],
        in_specs=smem(1) + vmem(4),
        out_specs=vmem(4),
        scratch_shapes=[pltpu.VMEM((3, 4 * rows, quarter, nz), f32)],
        compiler_params=small,
        name="gather",
    )(offsets, own, *received)
    arrived = [passed_along(p, "tile", rel) for rel, p in zip((1, 2, 3), parts)]
    return tuple(
        pl.pallas_call(
            functools.partial(finish_kernel, rows),
            out_shape=[jax.ShapeDtypeStruct((rows, quarter, nz), f32)] * 3,
            in_specs=vmem(4),
            out_specs=vmem(3),
            compiler_params=small,
            name="finish",
        )(here, *arrived)
    )


def solution(mesh):
    placed = (
        P(("groups", "tile"), None, None),
        P(("groups", "tile"), None, None),
        P(("groups", "tile"), None, None),
        P(("groups", "tile"), None, None),
        P(("groups", "shot"), None, "tile", None, None),
        P(("groups", "shot"), None, "tile", None, None),
        P(("groups", "shot")),
        P(("groups", "shot")),
        P(("groups", "shot"), None),
        P(("groups", "shot"), None),
        P(("groups", "shot"), None, None),
    )
    return jax.shard_map(
        on_device,
        mesh=mesh,
        in_specs=placed,
        out_specs=(
            P(("groups", "tile"), "shot", None),
            P(("groups", "tile"), "shot", None),
            P(("groups", "tile"), "shot", None),
        ),
        check_vma=False,
    )
```

```python
import functools

import jax
import jax.numpy as jnp
from jax import lax
from jax.experimental import pallas as pl
from jax.experimental.pallas import tpu as pltpu
from jax.sharding import PartitionSpec as P

TOP = 32767.0
PAD = 8
UNROLL = 4
SHORT = pl.CostEstimate(flops=0, bytes_accessed=1024, transcendentals=0)
EARLY = pl.CostEstimate(flops=0, bytes_accessed=16 * 1024 * 1024, transcendentals=0)
STATE_BOUND = 2.0


def passed_along(x, axis, by):
    count = lax.axis_size(axis)
    return lax.ppermute(x, axis, [(i, (i + by) % count) for i in range(count)])


def swapped(x, mask):
    count = lax.axis_size("shot")
    return lax.ppermute(x, "shot", [(i, i ^ mask) for i in range(count)])


def encoded(x, inverse):
    root = jnp.sqrt(jnp.sqrt(jnp.abs(x) * inverse))
    level = jnp.minimum(root * TOP + 0.5, TOP)
    return jnp.where(x < 0, -level, level).astype(jnp.int32).astype(jnp.int16)


def decoded(code, scale):
    level = code.astype(jnp.int32).astype(jnp.float32) * (1.0 / TOP)
    square = level * level
    value = square * square * scale
    return jnp.where(level < 0, -value, value)


def power_of(blocks):
    top = functools.reduce(jnp.maximum, [jnp.max(jnp.abs(x), axis=0) for x in blocks])
    top = jnp.max(jnp.max(top, axis=0, keepdims=True), axis=1, keepdims=True)
    return jnp.ceil(jnp.log2(jnp.maximum(top, 1e-30))) + 1.0


def head_row(powers, lines, offset):
    line = lax.broadcasted_iota(jnp.int32, (lines, 128), 0)
    head = jnp.full((lines, 128), offset, jnp.int32)
    for n, power in enumerate(powers):
        head = jnp.where(line == n, jnp.broadcast_to(power, (lines, 128)).astype(jnp.int32), head)
    return head.astype(jnp.int16)


def scales_of(head):
    return [jnp.exp2(head[n:n + 1]) for n in range(3)]


def tiled(x):
    return x.reshape(x.shape[:-2] + (x.shape[-2] // 8, 8, x.shape[-1]))


def vmem(count):
    return [pl.BlockSpec(memory_space=pltpu.VMEM)] * count


def smem(count):
    return [pl.BlockSpec(memory_space=pltpu.SMEM)] * count


def anywhere(count):
    return [pl.BlockSpec(memory_space=pl.ANY)] * count


def edges_kernel(widths, fwd, adj, up, down):
    rows = fwd.shape[2]
    n = 0
    for state, width in zip((fwd, adj), widths):
        for field in range(2):
            for i in range(width):
                up[n] = encoded(state[0, field, rows - width + i], 1.0 / STATE_BOUND)
                down[n] = encoded(state[0, field, i], 1.0 / STATE_BOUND)
                n += 1


def receivers_kernel(steps, ext, rows, tiles, rec, observed, out):
    span, ny, nz = out.shape[1:]
    count = rec.shape[1]
    nx = rows * tiles
    first = lax.axis_index("tile") * rows - ext
    cells = rec[...]
    plane = ny * nz
    x = cells // plane - first
    x = jnp.where(x < 0, x + nx, x)
    x = jnp.where(x >= nx, x - nx, x)
    line = x * ny + (cells // nz) % ny
    depth = cells % nz
    hit = lax.broadcasted_iota(jnp.int32, (span * ny, count), 0) == line
    hit = jnp.where(hit, 1.0, 0.0).astype(jnp.bfloat16)
    column = lax.broadcasted_iota(jnp.int32, (nz, count), 0) == depth

    def dense(weights):
        dims = (((1,), (1,)), ((), ()))
        return lax.dot_general(hit, weights, dims, preferred_element_type=jnp.float32).reshape(span, ny, nz)

    out[0] = dense(jnp.where(column, 1.0, 0.0).astype(jnp.bfloat16))
    for k in range(steps):
        rest = jnp.where(column, observed[0, k:k + 1, :], 0.0)
        total = None
        for _ in range(3):
            term = rest.astype(jnp.bfloat16)
            rest = rest - term.astype(jnp.float32)
            total = dense(term) if total is None else total + dense(term)
        out[k + 1] = total


def sin_cos(t):
    u = t * t
    s = 1.0 / 6227020800.0
    for c in (-1.0 / 39916800.0, 1.0 / 362880.0, -1.0 / 5040.0, 1.0 / 120.0, -1.0 / 6.0, 1.0):
        s = s * u + c
    s = s * t
    c = 1.0 / 479001600.0
    for d in (-1.0 / 3628800.0, 1.0 / 40320.0, -1.0 / 720.0, 1.0 / 24.0, -0.5, 1.0):
        c = c * u + d
    return s, c


def coefficients_kernel(ext, coded, n_model, offset_ref, *refs):
    model_refs, (vsq, ge, gd, s2, sc, va_own) = refs[:n_model], refs[n_model:n_model + 6]
    model, sem = refs[n_model + 6:]
    rows, ny, nz = va_own.shape
    total = rows + 2 * ext
    copies = []
    if coded:
        j = lax.axis_index("shot")
        for index, ref in enumerate(model_refs):
            if index == 0:
                target = model.at[:, 0]
            else:
                target = model.at[j ^ ((index - 1) % 4), (index - 1) // 4 + 1]
            copies.append(pltpu.make_async_copy(ref, target, sem))
    else:
        for rel, ref in enumerate(model_refs):
            for field in range(4):
                copies.append(pltpu.make_async_copy(ref.at[field], model.at[field, rel], sem))
    for copy in copies:
        copy.start()
    for copy in copies:
        copy.wait()
    offset = offset_ref[0]
    around = rows * 4

    def model_row(n, i):
        at = lax.rem(i - ext + offset + around, around)
        return model[n, lax.div(at, rows), lax.rem(at, rows)].astype(jnp.float32).reshape(ny, nz)

    @pl.loop(1, total - 1, unroll=10)
    def _(i):
        va, eps, dlt, angle = (model_row(n, i) for n in range(4))
        sine, cosine = sin_cos(angle)
        vsq[i] = va * va
        ge[i] = 1.0 + 2.0 * eps
        gd[i] = 1.0 + 2.0 * dlt
        s2[i] = sine * sine
        sc[i] = 0.5 * sine * cosine

    @pl.loop(0, rows, unroll=UNROLL)
    def _(i):
        va_own[i] = model_row(0, i + ext)


class Stencils:
    def __init__(self, ny, nz, sums, slopes):
        self.nz, self.sums, self.slopes = nz, sums, slopes
        self.inner = slice(PAD, PAD + ny)
        self.up_one = slice(PAD - 1, PAD + ny - 1)
        self.down_one = slice(PAD + 1, PAD + ny + 1)
        lane = lax.broadcasted_iota(jnp.int32, (ny, nz), 1)
        self.not_first, self.not_last = lane > 0, lane < nz - 1

    def sum_and_slope(self, row):
        lines = row.shape[0]
        above = jnp.where(self.not_last[:lines], pltpu.roll(row, self.nz - 1, 1), 0.0)
        below = jnp.where(self.not_first[:lines], pltpu.roll(row, 1, 1), 0.0)
        return above + below, above - below

    def store_depth(self, turn, field, where, row):
        self.sums[turn][field][where], self.slopes[turn][field][where] = self.sum_and_slope(row)

    def crossed(self, turn, field, i):
        return self.slopes[turn][field][i + 1] - self.slopes[turn][field][i - 1]

    def flat(self, turn, ref, i, a2, c2, ab):
        side = ref[i - 1, self.inner] + ref[i + 1, self.inner]
        beside = ref[i, self.up_one] + ref[i, self.down_one]
        depth = a2 * self.sums[turn][0][i] - ab * self.crossed(turn, 0, i)
        return (c2 * side + beside - 4.0 * ref[i, self.inner]) + depth

    def steep(self, turn, ref, i, a2, c2, ab):
        side = ref[i - 1] + ref[i + 1]
        return (a2 * side - 2.0 * ref[i]) + (c2 * self.sums[turn][1][i] + ab * self.crossed(turn, 1, i))


def clear_edges(refs, total, ny):
    edge = jnp.zeros((PAD, refs[0].shape[2]), jnp.float32)

    @pl.loop(0, total, unroll=total)
    def _(i):
        for ref in refs:
            ref[i, 0:PAD] = edge
            ref[i, PAD + ny:] = edge


def forward_kernel(steps, ext, tiles, source_ref, wavelet_ref, vsq, ge, gd, s2, sc, dense, fwd, f_lo, f_hi, *refs):
    it = iter(refs)
    kept_h, kept_v, resid = next(it), next(it), next(it)
    press, shear = ([next(it) for _ in range(steps + 1)] for _ in range(2))
    sums, slopes = ([[next(it) for _ in range(2)] for _ in range(2)] for _ in range(2))
    code, sem, sem_code = it
    rows, ny, nz = fwd.shape[2:]
    total = rows + 2 * ext
    near = steps - 1
    copies = [
        pltpu.make_async_copy(fwd.at[0, 0], press[0].at[pl.ds(ext, rows), pl.ds(PAD, ny)], sem),
        pltpu.make_async_copy(fwd.at[0, 1], shear[0].at[pl.ds(ext, rows)], sem),
    ]
    code_copies = [
        pltpu.make_async_copy(f_lo.at[pl.ds(0, 2 * ext)], code.at[0], sem_code),
        pltpu.make_async_copy(f_hi.at[pl.ds(0, 2 * ext)], code.at[1], sem_code),
    ]
    for copy in code_copies + copies:
        copy.start()
    clear_edges(press[:steps], total, ny)
    ops = Stencils(ny, nz, sums, slopes)
    inner = ops.inner
    for copy in code_copies:
        copy.wait()

    @pl.loop(0, ext, unroll=7)
    def _(i):
        for side, base in ((0, 0), (1, ext + rows)):
            p = decoded(code[side, i], STATE_BOUND).reshape(ny, nz)
            q = decoded(code[side, ext + i], STATE_BOUND).reshape(ny, nz)
            press[0][base + i, inner] = p
            shear[0][base + i] = q
            ops.store_depth(0, 0, base + i, p)
            ops.store_depth(0, 1, base + i, q)

    for copy in copies:
        copy.wait()

    @pl.loop(ext, ext + rows, unroll=8)
    def _(i):
        ops.store_depth(0, 0, i, press[0][i, inner])
        ops.store_depth(0, 1, i, shear[0][i])

    tile_first = lax.axis_index("tile") * rows
    nx = rows * tiles
    cell = source_ref[0]
    src_row = lax.rem(lax.div(cell, ny * nz) - tile_first + ext + nx, nx)
    src_y = lax.rem(lax.div(cell, nz), ny)
    src_here = lax.broadcasted_iota(jnp.int32, (1, nz), 1) == lax.rem(cell, nz)

    for k in range(steps):
        turn, last = k % 2, k == steps - 1
        p_new, q_new = press[k + 1], shear[k + 1]

        def one_row(i, keep):
            a2, ab = s2[i], sc[i]
            c2 = 1.0 - a2
            hp = ops.flat(turn, press[k], i, a2, c2, ab)
            hq = ops.steep(turn, shear[k], i, a2, c2, ab)
            if keep:
                kept_h[k, i - ext] = hp
                kept_v[k, i - ext] = hq
            p, q = press[k][i, inner], shear[k][i]
            speed = vsq[i]
            p_base = 2.0 * p - press[k - 1][i, inner] if k else p
            q_base = 2.0 * q - shear[k - 1][i] if k else q
            p = p_base + speed * (ge[i] * hp + hq)
            q = q_base + speed * (gd[i] * hp + hq)
            p_new[i, inner] = p
            q_new[i] = q
            if not last:
                ops.store_depth(1 - turn, 0, i, p)
                ops.store_depth(1 - turn, 1, i, q)

        @pl.loop(1 + k, ext, unroll=ext - 1 - k)
        def _(i):
            one_row(i, False)
            one_row(total - 1 - i, False)

        pl.loop(ext, ext + rows, unroll=8)(lambda i: one_row(i, True))

        @pl.when((src_row >= 1 + k) & (src_row < total - 1 - k))
        def _():
            amount = jnp.where(src_here, wavelet_ref[0, k], 0.0)
            line = pl.ds(src_y, 1)
            p = p_new[src_row, pl.ds(PAD + src_y, 1)] + amount
            q = q_new[src_row, line] + amount
            p_new[src_row, pl.ds(PAD + src_y, 1)] = p
            q_new[src_row, line] = q
            if not last:
                for field, row in enumerate((p, q)):
                    total_row, slope_row = ops.sum_and_slope(row)
                    sums[1 - turn][field][src_row, line] = total_row
                    slopes[1 - turn][field][src_row, line] = slope_row

        @pl.loop(near - k, near + rows + k, unroll=rows + 2 * k)
        def _(r):
            resid[k, r] = dense[0, r] * p_new[r + ext - near, inner] - dense[k + 1, r]


def adjoint_kernel(steps, ext, coded, offset_ref, vsq, ge, gd, s2, sc, va, kept_h, kept_v, resid, adj, a_lo, a_hi, *refs):
    it = iter(refs)
    outs = [next(it) for _ in range(4 if coded else 1)]
    lam, mu = ([next(it) for _ in range(steps + 1)] for _ in range(2))
    sums, slopes = ([[next(it) for _ in range(2)]] for _ in range(2))
    w1, w2, grads, code, sem, sem_code = it
    rows, ny, nz = adj.shape[2:]
    low_c = ext - steps
    total = rows + 2 * steps
    copies = [
        pltpu.make_async_copy(adj.at[0, 0], lam[0].at[pl.ds(steps, rows)], sem),
        pltpu.make_async_copy(adj.at[0, 1], mu[0].at[pl.ds(steps, rows)], sem),
    ]
    code_copies = [
        pltpu.make_async_copy(a_lo.at[pl.ds(2 * ext, 2 * steps)], code.at[0], sem_code),
        pltpu.make_async_copy(a_hi.at[pl.ds(2 * ext, 2 * steps)], code.at[1], sem_code),
    ]
    for copy in code_copies + copies:
        copy.start()
    clear_edges([w1], total, ny)
    ops = Stencils(ny, nz, sums, slopes)
    inner = ops.inner
    for copy in code_copies:
        copy.wait()

    @pl.loop(0, steps, unroll=4)
    def _(i):
        for side, base in ((0, 0), (1, steps + rows)):
            lam[0][base + i] = decoded(code[side, i], STATE_BOUND).reshape(ny, nz)
            mu[0][base + i] = decoded(code[side, steps + i], STATE_BOUND).reshape(ny, nz)

    for copy in copies:
        copy.wait()

    for a in range(steps):
        k = steps - 1 - a

        @pl.loop(a, total - a, unroll=total - 2 * a)
        def _(i):
            l, m = lam[a][i], mu[a][i]
            c = i + low_c
            speed = vsq[c]
            first = speed * (ge[c] * l + gd[c] * m)
            second = speed * (l + m)
            w1[i, inner] = first
            w2[i] = second
            ops.store_depth(0, 0, i, first)
            ops.store_depth(0, 1, i, second)

        @pl.loop(a + 1, total - a - 1, unroll=total - 2 * a - 2)
        def _(i):
            c = i + low_c
            a2, ab = s2[c], sc[c]
            c2 = 1.0 - a2
            h = ops.flat(0, w1, i, a2, c2, ab)
            v = ops.steep(0, w2, i, a2, c2, ab)
            l, m = lam[a][i], mu[a][i]
            l_base = 2.0 * l - lam[a - 1][i] if a else l
            m_base = 2.0 * m - mu[a - 1][i] if a else m
            lam[a + 1][i] = l_base + h + resid[k, i - 1]
            mu[a + 1][i] = m_base + v

    @pl.loop(0, rows, unroll=8)
    def _(r):
        sum_e = sum_d = sum_v = 0.0
        for k in range(steps):
            l, m = lam[steps - k][r + steps], mu[steps - k][r + steps]
            hp, hq = kept_h[k, r], kept_v[k, r]
            sum_e = sum_e + l * hp
            sum_d = sum_d + m * hp
            sum_v = sum_v + (l + m) * hq
        c = r + ext
        twice, twice_sq = 2.0 * va[r], 2.0 * vsq[c]
        grads[0, r] = twice * (ge[c] * sum_e + gd[c] * sum_d + sum_v)
        grads[1, r] = twice_sq * sum_e
        grads[2, r] = twice_sq * sum_d

    if not coded:
        outs[0][...] = grads[...]
        return
    quarter = ny // 4
    j = lax.axis_index("shot")
    powers = [power_of([grads[n]]) for n in range(3)]
    head = head_row(powers, quarter, offset_ref[0])
    for mask in range(4):
        y0 = pl.multiple_of((j ^ mask) * quarter, quarter)
        for n in range(3):
            part = grads[n, :, pl.ds(y0, quarter)]
            if mask:
                outs[mask][n * rows:(n + 1) * rows] = encoded(part, jnp.exp2(-powers[n]))
            else:
                outs[0][n * rows:(n + 1) * rows] = part
        if mask:
            outs[mask][3 * rows] = head


def gather_kernel(rows, offset_ref, own, *refs):
    codes, (here, *outs), acc = refs[:3], refs[3:7], refs[7]
    around = 4 * rows
    quarter, nz = own.shape[1:]
    zero = jnp.zeros((quarter, nz), jnp.float32)

    @pl.loop(0, around, unroll=8)
    def _(x):
        for n in range(3):
            acc[n, x] = zero

    offset = offset_ref[0]

    for r in range(rows):
        for n in range(3):
            acc[n, lax.rem(r + offset, around)] = own[n * rows + r]

    for code in codes:
        head = code[3 * rows].astype(jnp.int32).astype(jnp.float32)
        theirs = jnp.max(head[8:9]).astype(jnp.int32)
        scales = scales_of(head)
        for n in range(3):
            part = decoded(code[n * rows:(n + 1) * rows], scales[n])
            for r in range(rows):
                acc[n, lax.rem(r + theirs, around)] += part[r]

    here[...] = acc[:, 0:rows].reshape(here.shape)
    for rel in range(1, 4):
        parts = [acc[n, rel * rows:(rel + 1) * rows] for n in range(3)]
        powers = [power_of([part]) for part in parts]
        for n in range(3):
            outs[rel - 1][n * rows:(n + 1) * rows] = encoded(parts[n], jnp.exp2(-powers[n]))
        outs[rel - 1][3 * rows] = head_row(powers, quarter, 0)


def finish_kernel(rows, own, *refs):
    codes, outs = refs[:3], refs[3:]
    scales = [scales_of(code[3 * rows].astype(jnp.int32).astype(jnp.float32)) for code in codes]
    for n in range(3):
        total = own[n * rows:(n + 1) * rows]
        for code, scale in zip(codes, scales):
            total = total + decoded(code[n * rows:(n + 1) * rows], scale[n])
        outs[n][...] = total


def on_device(
    velocity,
    epsilon,
    delta,
    tilt,
    forward_state,
    adjoint_state,
    offsets,
    src_cells,
    rec_cells,
    wavelet,
    observed,
):
    rows, ny, nz = velocity.shape
    tiles = lax.axis_size("tile")
    shots = lax.axis_size("shot")
    steps = wavelet.shape[1]
    ext = 2 * steps - 1
    near = steps - 1
    total = rows + 2 * ext
    span = rows + 2 * near
    assert rows >= ext
    coded = tiles == 4 and shots == 4
    f32, i16 = jnp.float32, jnp.int16

    small = pltpu.CompilerParams(vmem_limit_bytes=4 * 1024 * 1024)

    def struct(*shape, dtype=f32):
        return jax.ShapeDtypeStruct(shape, dtype)

    codes = pl.pallas_call(
        functools.partial(edges_kernel, (ext, steps)),
        out_shape=[struct(2 * (ext + steps), ny, nz, dtype=i16)] * 2,
        in_specs=vmem(2),
        out_specs=vmem(2),
        compiler_params=small,
        cost_estimate=EARLY,
        name="edges",
    )(forward_state, adjoint_state)

    def to_neighbours(up, down):
        return passed_along(up, "tile", 1), passed_along(down, "tile", -1)

    if coded:
        share = lax.select_n(lax.axis_index("shot"), velocity, epsilon, delta, tilt)
        ahead = passed_along(share, "tile", -1)
        behind = passed_along(share, "tile", 1)
        own = jnp.stack([velocity, epsilon, delta, tilt])
        ahead, behind, codes, own = lax.optimization_barrier((ahead, behind, codes, own))
        across = passed_along(ahead, "tile", -1)
        halo_lo, halo_hi = to_neighbours(*codes)
        far_ahead, far_behind, far_across = (swapped(piece, 2) for piece in (ahead, behind, across))
        model_refs = [own]
        for piece, other in ((ahead, far_ahead), (across, far_across), (behind, far_behind)):
            model_refs += [piece, swapped(piece, 1), other, swapped(other, 1)]
        shift = offsets
    else:
        nbits = max(1, (tiles - 1).bit_length())
        block = jnp.stack([velocity, epsilon, delta, tilt])
        whole = offsets[0] // rows
        for bit in range(nbits):
            moved = passed_along(block, "tile", -(1 << bit))
            block = jnp.where(jnp.bitwise_and(jnp.right_shift(whole, bit), 1) == 1, moved, block)
        model_refs = [block] + [passed_along(block, "tile", -by) for by in (1, 2, -1)]
        halo_lo, halo_hi = to_neighbours(*codes)
        shift = offsets % rows

    field = (total, ny, nz)
    *coefficients, va = pl.pallas_call(
        functools.partial(coefficients_kernel, ext, coded, len(model_refs)),
        out_shape=[struct(*field)] * 5 + [struct(rows, ny, nz)],
        in_specs=smem(1) + anywhere(len(model_refs)),
        out_specs=vmem(6),
        scratch_shapes=[
            pltpu.VMEM((4, 4, rows, ny // 8, 8, nz), jnp.bfloat16),
            pltpu.SemaphoreType.DMA,
        ],
        compiler_params=pltpu.CompilerParams(vmem_limit_bytes=16 * 1024 * 1024),
        cost_estimate=SHORT,
        name="coefficients",
    )(shift, *map(tiled, model_refs))

    cells, coefficients[0] = lax.optimization_barrier((rec_cells, coefficients[0]))
    dense = pl.pallas_call(
        functools.partial(receivers_kernel, steps, near, rows, tiles),
        out_shape=struct(steps + 1, span, ny, nz),
        in_specs=vmem(2),
        out_specs=pl.BlockSpec(memory_space=pltpu.VMEM),
        compiler_params=pltpu.CompilerParams(vmem_limit_bytes=8 * 1024 * 1024),
        cost_estimate=SHORT,
        name="receivers",
    )(cells, observed)

    kept_h, kept_v, resid = pl.pallas_call(
        functools.partial(forward_kernel, steps, ext, tiles),
        out_shape=[struct(steps, rows, ny, nz)] * 2 + [struct(steps, span, ny, nz)],
        in_specs=smem(2) + vmem(6) + anywhere(3),
        out_specs=vmem(3),
        scratch_shapes=[
            *[pltpu.VMEM((total, ny + 2 * PAD, nz), f32)] * (steps + 1),
            *[pltpu.VMEM(field, f32)] * (steps + 1 + 8),
            pltpu.VMEM((2, 2 * ext, ny // 8, 8, nz), i16),
            *[pltpu.SemaphoreType.DMA] * 2,
        ],
        compiler_params=pltpu.CompilerParams(vmem_limit_bytes=32 * 1024 * 1024),
        name="forward",
    )(src_cells, wavelet, *coefficients, dense, forward_state, *map(tiled, (halo_lo, halo_hi)))

    quarter = ny // 4
    if coded:
        wave_outs = [struct(3 * rows, quarter, nz)] + [struct(3 * rows + 1, quarter, nz, dtype=i16)] * 3
    else:
        wave_outs = [struct(3, rows, ny, nz)]
    narrow = (rows + 2 * steps, ny, nz)
    waves = pl.pallas_call(
        functools.partial(adjoint_kernel, steps, ext, coded),
        out_shape=wave_outs,
        in_specs=smem(1) + vmem(9) + anywhere(3),
        out_specs=vmem(len(wave_outs)),
        scratch_shapes=[
            *[pltpu.VMEM(narrow, f32)] * (2 * (steps + 1) + 4),
            pltpu.VMEM((rows + 2 * steps, ny + 2 * PAD, nz), f32),
            pltpu.VMEM(narrow, f32),
            pltpu.VMEM((3, rows, ny, nz), f32),
            pltpu.VMEM((2, 2 * steps, ny // 8, 8, nz), i16),
            *[pltpu.SemaphoreType.DMA] * 2,
        ],
        compiler_params=pltpu.CompilerParams(vmem_limit_bytes=24 * 1024 * 1024),
        name="adjoint",
    )(offsets, *coefficients, va, kept_h, kept_v, resid, adjoint_state, *map(tiled, (halo_lo, halo_hi)))

    if not coded:
        (gradients,) = waves
        within = shift[0]
        spread = jnp.zeros((3, 2 * rows, ny, nz), f32)
        spread = lax.dynamic_update_slice_in_dim(spread, gradients, within, 1)
        combined = spread[:, :rows] + passed_along(spread[:, rows:], "tile", 1)
        for bit in range(nbits):
            moved = passed_along(combined, "tile", 1 << bit)
            combined = jnp.where(jnp.bitwise_and(jnp.right_shift(whole, bit), 1) == 1, moved, combined)
        summed = lax.psum(combined, "shot")
        share = ny // shots
        result = lax.dynamic_slice_in_dim(summed, lax.axis_index("shot") * share, share, 2)
        return (result[0], result[1], result[2])

    own, *sent = waves
    received = [swapped(code, mask) for mask, code in zip((1, 2, 3), sent)]
    part = struct(3 * rows + 1, quarter, nz, dtype=i16)
    here, *parts = pl.pallas_call(
        functools.partial(gather_kernel, rows),
        out_shape=[jax.ShapeDtypeStruct((3 * rows, quarter, nz), f32), part, part, part],
        in_specs=smem(1) + vmem(4),
        out_specs=vmem(4),
        scratch_shapes=[pltpu.VMEM((3, 4 * rows, quarter, nz), f32)],
        compiler_params=small,
        name="gather",
    )(offsets, own, *received)
    arrived = [passed_along(p, "tile", rel) for rel, p in zip((1, 2, 3), parts)]
    return tuple(
        pl.pallas_call(
            functools.partial(finish_kernel, rows),
            out_shape=[jax.ShapeDtypeStruct((rows, quarter, nz), f32)] * 3,
            in_specs=vmem(4),
            out_specs=vmem(3),
            compiler_params=small,
            name="finish",
        )(here, *arrived)
    )


def solution(mesh):
    placed = (
        P(("groups", "tile"), None, None),
        P(("groups", "tile"), None, None),
        P(("groups", "tile"), None, None),
        P(("groups", "tile"), None, None),
        P(("groups", "shot"), None, "tile", None, None),
        P(("groups", "shot"), None, "tile", None, None),
        P(("groups", "shot")),
        P(("groups", "shot")),
        P(("groups", "shot"), None),
        P(("groups", "shot"), None),
        P(("groups", "shot"), None, None),
    )
    return jax.shard_map(
        on_device,
        mesh=mesh,
        in_specs=placed,
        out_specs=(
            P(("groups", "tile"), "shot", None),
            P(("groups", "tile"), "shot", None),
            P(("groups", "tile"), "shot", None),
        ),
        check_vma=False,
    )
```

```python
import functools

import jax
import jax.numpy as jnp
from jax import lax
from jax.experimental import pallas as pl
from jax.experimental.pallas import tpu as pltpu
from jax.sharding import PartitionSpec as P

TOP = 32767.0
PAD = 8
UNROLL = 4
SHORT = pl.CostEstimate(flops=0, bytes_accessed=1024, transcendentals=0)
EARLY = pl.CostEstimate(flops=0, bytes_accessed=16 * 1024 * 1024, transcendentals=0)
STATE_BOUND = 2.0


def passed_along(x, axis, by):
    count = lax.axis_size(axis)
    return lax.ppermute(x, axis, [(i, (i + by) % count) for i in range(count)])


def swapped(x, mask):
    count = lax.axis_size("shot")
    return lax.ppermute(x, "shot", [(i, i ^ mask) for i in range(count)])


def encoded(x, inverse):
    root = jnp.sqrt(jnp.sqrt(jnp.abs(x) * inverse))
    level = jnp.minimum(root * TOP + 0.5, TOP)
    return jnp.where(x < 0, -level, level).astype(jnp.int32).astype(jnp.int16)


def decoded(code, scale):
    level = code.astype(jnp.int32).astype(jnp.float32) * (1.0 / TOP)
    square = level * level
    value = square * square * scale
    return jnp.where(level < 0, -value, value)


def power_of(blocks):
    top = functools.reduce(jnp.maximum, [jnp.max(jnp.abs(x), axis=0) for x in blocks])
    top = jnp.max(jnp.max(top, axis=0, keepdims=True), axis=1, keepdims=True)
    return jnp.ceil(jnp.log2(jnp.maximum(top, 1e-30))) + 1.0


def head_row(powers, lines, offset):
    line = lax.broadcasted_iota(jnp.int32, (lines, 128), 0)
    head = jnp.full((lines, 128), offset, jnp.int32)
    for n, power in enumerate(powers):
        head = jnp.where(line == n, jnp.broadcast_to(power, (lines, 128)).astype(jnp.int32), head)
    return head.astype(jnp.int16)


def scales_of(head):
    return [jnp.exp2(head[n:n + 1]) for n in range(3)]


def tiled(x):
    return x.reshape(x.shape[:-2] + (x.shape[-2] // 8, 8, x.shape[-1]))


def vmem(count):
    return [pl.BlockSpec(memory_space=pltpu.VMEM)] * count


def smem(count):
    return [pl.BlockSpec(memory_space=pltpu.SMEM)] * count


def anywhere(count):
    return [pl.BlockSpec(memory_space=pl.ANY)] * count


def edges_kernel(widths, fwd, adj, up, down):
    rows = fwd.shape[2]
    n = 0
    for state, width in zip((fwd, adj), widths):
        for field in range(2):
            for i in range(width):
                up[n] = encoded(state[0, field, rows - width + i], 1.0 / STATE_BOUND)
                down[n] = encoded(state[0, field, i], 1.0 / STATE_BOUND)
                n += 1


def receivers_kernel(steps, ext, rows, tiles, rec, observed, out):
    span, ny, nz = out.shape[1:]
    count = rec.shape[1]
    nx = rows * tiles
    first = lax.axis_index("tile") * rows - ext
    cells = rec[...]
    plane = ny * nz
    x = cells // plane - first
    x = jnp.where(x < 0, x + nx, x)
    x = jnp.where(x >= nx, x - nx, x)
    line = x * ny + (cells // nz) % ny
    depth = cells % nz
    hit = lax.broadcasted_iota(jnp.int32, (span * ny, count), 0) == line
    hit = jnp.where(hit, 1.0, 0.0).astype(jnp.bfloat16)
    column = lax.broadcasted_iota(jnp.int32, (nz, count), 0) == depth

    def dense(weights):
        dims = (((1,), (1,)), ((), ()))
        return lax.dot_general(hit, weights, dims, preferred_element_type=jnp.float32).reshape(span, ny, nz)

    out[0] = dense(jnp.where(column, 1.0, 0.0).astype(jnp.bfloat16))
    for k in range(steps):
        rest = jnp.where(column, observed[0, k:k + 1, :], 0.0)
        total = None
        for _ in range(3):
            term = rest.astype(jnp.bfloat16)
            rest = rest - term.astype(jnp.float32)
            total = dense(term) if total is None else total + dense(term)
        out[k + 1] = total


def sin_cos(t):
    u = t * t
    s = 1.0 / 6227020800.0
    for c in (-1.0 / 39916800.0, 1.0 / 362880.0, -1.0 / 5040.0, 1.0 / 120.0, -1.0 / 6.0, 1.0):
        s = s * u + c
    s = s * t
    c = 1.0 / 479001600.0
    for d in (-1.0 / 3628800.0, 1.0 / 40320.0, -1.0 / 720.0, 1.0 / 24.0, -0.5, 1.0):
        c = c * u + d
    return s, c


def coefficients_kernel(ext, coded, n_model, offset_ref, *refs):
    model_refs, (vsq, vge, vgd, s2, sc, va_own, ge_own, gd_own) = refs[:n_model], refs[n_model:n_model + 8]
    model, sem = refs[n_model + 8:]
    rows, ny, nz = va_own.shape
    total = rows + 2 * ext
    copies = []
    if coded:
        j = lax.axis_index("shot")
        for index, ref in enumerate(model_refs):
            if index == 0:
                target = model.at[:, 0]
            else:
                target = model.at[j ^ ((index - 1) % 4), (index - 1) // 4 + 1]
            copies.append(pltpu.make_async_copy(ref, target, sem))
    else:
        for rel, ref in enumerate(model_refs):
            for field in range(4):
                copies.append(pltpu.make_async_copy(ref.at[field], model.at[field, rel], sem))
    for copy in copies:
        copy.start()
    for copy in copies:
        copy.wait()
    offset = offset_ref[0]
    around = rows * 4

    def model_row(n, i):
        at = lax.rem(i - ext + offset + around, around)
        return model[n, lax.div(at, rows), lax.rem(at, rows)].astype(jnp.float32).reshape(ny, nz)

    @pl.loop(1, total - 1, unroll=10)
    def _(i):
        va, eps, dlt, angle = (model_row(n, i) for n in range(4))
        sine, cosine = sin_cos(angle)
        square = va * va
        vsq[i] = square
        vge[i] = square * (1.0 + 2.0 * eps)
        vgd[i] = square * (1.0 + 2.0 * dlt)
        s2[i] = sine * sine
        sc[i] = 0.5 * sine * cosine

    @pl.loop(0, rows, unroll=UNROLL)
    def _(i):
        va_own[i] = model_row(0, i + ext)
        ge_own[i] = 1.0 + 2.0 * model_row(1, i + ext)
        gd_own[i] = 1.0 + 2.0 * model_row(2, i + ext)


class Stencils:
    def __init__(self, ny, nz, sums, slopes):
        self.nz, self.sums, self.slopes = nz, sums, slopes
        self.inner = slice(PAD, PAD + ny)
        self.up_one = slice(PAD - 1, PAD + ny - 1)
        self.down_one = slice(PAD + 1, PAD + ny + 1)
        lane = lax.broadcasted_iota(jnp.int32, (ny, nz), 1)
        self.not_first, self.not_last = lane > 0, lane < nz - 1

    def sum_and_slope(self, row):
        lines = row.shape[0]
        above = jnp.where(self.not_last[:lines], pltpu.roll(row, self.nz - 1, 1), 0.0)
        below = jnp.where(self.not_first[:lines], pltpu.roll(row, 1, 1), 0.0)
        return above + below, above - below

    def store_depth(self, turn, field, where, row):
        self.sums[turn][field][where], self.slopes[turn][field][where] = self.sum_and_slope(row)

    def crossed(self, turn, field, i):
        return self.slopes[turn][field][i + 1] - self.slopes[turn][field][i - 1]

    def flat(self, turn, ref, i, a2, c2, ab):
        side = ref[i - 1, self.inner] + ref[i + 1, self.inner]
        beside = ref[i, self.up_one] + ref[i, self.down_one]
        depth = a2 * self.sums[turn][0][i] - ab * self.crossed(turn, 0, i)
        return (c2 * side + beside - 4.0 * ref[i, self.inner]) + depth

    def steep(self, turn, ref, i, a2, c2, ab):
        side = ref[i - 1] + ref[i + 1]
        return (a2 * side - 2.0 * ref[i]) + (c2 * self.sums[turn][1][i] + ab * self.crossed(turn, 1, i))


def clear_edges(refs, total, ny):
    edge = jnp.zeros((PAD, refs[0].shape[2]), jnp.float32)

    @pl.loop(0, total, unroll=total)
    def _(i):
        for ref in refs:
            ref[i, 0:PAD] = edge
            ref[i, PAD + ny:] = edge


def forward_kernel(steps, ext, tiles, source_ref, wavelet_ref, vsq, vge, vgd, s2, sc, dense, fwd, f_lo, f_hi, *refs):
    it = iter(refs)
    kept_h, kept_v, resid = next(it), next(it), next(it)
    press, shear = ([next(it) for _ in range(count)] for count in (steps + 1, steps))
    sums, slopes = ([[next(it) for _ in range(2)] for _ in range(2)] for _ in range(2))
    code, sem, sem_code = it
    rows, ny, nz = fwd.shape[2:]
    total = rows + 2 * ext
    near = steps - 1
    copies = [
        pltpu.make_async_copy(fwd.at[0, 0], press[0].at[pl.ds(ext, rows), pl.ds(PAD, ny)], sem),
        pltpu.make_async_copy(fwd.at[0, 1], shear[0].at[pl.ds(ext, rows)], sem),
    ]
    code_copies = [
        pltpu.make_async_copy(f_lo.at[pl.ds(0, 2 * ext)], code.at[0], sem_code),
        pltpu.make_async_copy(f_hi.at[pl.ds(0, 2 * ext)], code.at[1], sem_code),
    ]
    for copy in code_copies + copies:
        copy.start()
    clear_edges(press[:steps], total, ny)
    ops = Stencils(ny, nz, sums, slopes)
    inner = ops.inner
    for copy in code_copies:
        copy.wait()

    @pl.loop(0, ext, unroll=7)
    def _(i):
        for side, base in ((0, 0), (1, ext + rows)):
            p = decoded(code[side, i], STATE_BOUND).reshape(ny, nz)
            q = decoded(code[side, ext + i], STATE_BOUND).reshape(ny, nz)
            press[0][base + i, inner] = p
            shear[0][base + i] = q
            ops.store_depth(0, 0, base + i, p)
            ops.store_depth(0, 1, base + i, q)

    for copy in copies:
        copy.wait()

    @pl.loop(ext, ext + rows, unroll=8)
    def _(i):
        ops.store_depth(0, 0, i, press[0][i, inner])
        ops.store_depth(0, 1, i, shear[0][i])

    tile_first = lax.axis_index("tile") * rows
    nx = rows * tiles
    cell = source_ref[0]
    src_row = lax.rem(lax.div(cell, ny * nz) - tile_first + ext + nx, nx)
    src_y = lax.rem(lax.div(cell, nz), ny)
    depth = lax.broadcasted_iota(jnp.int32, (1, nz), 1) - lax.rem(cell, nz)
    src_here, src_above, src_below = depth == 0, depth == -1, depth == 1

    for k in range(steps):
        turn, last = k % 2, k == steps - 1
        p_new, q_new = press[k + 1], None if last else shear[k + 1]

        def one_row(i, keep):
            a2, ab = s2[i], sc[i]
            c2 = 1.0 - a2
            hp = ops.flat(turn, press[k], i, a2, c2, ab)
            hq = ops.steep(turn, shear[k], i, a2, c2, ab)
            if keep:
                kept_h[k, i - ext] = hp
                kept_v[k, i - ext] = hq
            steep_part = vsq[i] * hq
            p = press[k][i, inner]
            p_base = 2.0 * p - press[k - 1][i, inner] if k else p
            p = p_base + (vge[i] * hp + steep_part)
            p_new[i, inner] = p
            if last:
                return
            q = shear[k][i]
            q_base = 2.0 * q - shear[k - 1][i] if k else q
            q = q_base + (vgd[i] * hp + steep_part)
            q_new[i] = q
            ops.store_depth(1 - turn, 0, i, p)
            ops.store_depth(1 - turn, 1, i, q)

        @pl.loop(1 + k, ext, unroll=ext - 1 - k)
        def _(i):
            one_row(i, False)
            one_row(total - 1 - i, False)

        pl.loop(ext, ext + rows, unroll=8)(lambda i: one_row(i, True))

        @pl.when((src_row >= 1 + k) & (src_row < total - 1 - k))
        def _():
            amount = wavelet_ref[0, k]
            here, above, below = (jnp.where(mask, amount, 0.0) for mask in (src_here, src_above, src_below))
            line = pl.ds(src_y, 1)
            p_new[src_row, pl.ds(PAD + src_y, 1)] += here
            if not last:
                q_new[src_row, line] += here
                for field in range(2):
                    sums[1 - turn][field][src_row, line] += above + below
                    slopes[1 - turn][field][src_row, line] += above - below

        @pl.loop(near - k, near + rows + k, unroll=rows + 2 * k)
        def _(r):
            resid[k, r] = dense[0, r] * p_new[r + ext - near, inner] - dense[k + 1, r]


def adjoint_kernel(steps, ext, coded, offset_ref, vsq, vge, vgd, s2, sc, va, ge, gd, kept_h, kept_v, resid, adj, a_lo, a_hi, *refs):
    it = iter(refs)
    outs = [next(it) for _ in range(4 if coded else 1)]
    lam, mu = ([next(it) for _ in range(steps + 1)] for _ in range(2))
    sums, slopes = ([[next(it) for _ in range(2)]] for _ in range(2))
    w1, w2, grads, code, sem, sem_code = it
    rows, ny, nz = adj.shape[2:]
    low_c = ext - steps
    total = rows + 2 * steps
    copies = [
        pltpu.make_async_copy(adj.at[0, 0], lam[0].at[pl.ds(steps, rows)], sem),
        pltpu.make_async_copy(adj.at[0, 1], mu[0].at[pl.ds(steps, rows)], sem),
    ]
    code_copies = [
        pltpu.make_async_copy(a_lo.at[pl.ds(2 * ext, 2 * steps)], code.at[0], sem_code),
        pltpu.make_async_copy(a_hi.at[pl.ds(2 * ext, 2 * steps)], code.at[1], sem_code),
    ]
    for copy in code_copies + copies:
        copy.start()
    clear_edges([w1], total, ny)
    ops = Stencils(ny, nz, sums, slopes)
    inner = ops.inner
    for copy in code_copies:
        copy.wait()

    @pl.loop(0, steps, unroll=4)
    def _(i):
        for side, base in ((0, 0), (1, steps + rows)):
            lam[0][base + i] = decoded(code[side, i], STATE_BOUND).reshape(ny, nz)
            mu[0][base + i] = decoded(code[side, steps + i], STATE_BOUND).reshape(ny, nz)

    for copy in copies:
        copy.wait()

    for a in range(steps):
        k = steps - 1 - a

        @pl.loop(a, total - a, unroll=total - 2 * a)
        def _(i):
            l, m = lam[a][i], mu[a][i]
            c = i + low_c
            first = vge[c] * l + vgd[c] * m
            second = vsq[c] * (l + m)
            w1[i, inner] = first
            w2[i] = second
            ops.store_depth(0, 0, i, first)
            ops.store_depth(0, 1, i, second)

        @pl.loop(a + 1, total - a - 1, unroll=total - 2 * a - 2)
        def _(i):
            c = i + low_c
            a2, ab = s2[c], sc[c]
            c2 = 1.0 - a2
            h = ops.flat(0, w1, i, a2, c2, ab)
            v = ops.steep(0, w2, i, a2, c2, ab)
            l, m = lam[a][i], mu[a][i]
            l_base = 2.0 * l - lam[a - 1][i] if a else l
            m_base = 2.0 * m - mu[a - 1][i] if a else m
            lam[a + 1][i] = l_base + h + resid[k, i - 1]
            mu[a + 1][i] = m_base + v

    @pl.loop(0, rows, unroll=8)
    def _(r):
        sum_e = sum_d = sum_v = 0.0
        for k in range(steps):
            l, m = lam[steps - k][r + steps], mu[steps - k][r + steps]
            hp, hq = kept_h[k, r], kept_v[k, r]
            sum_e = sum_e + l * hp
            sum_d = sum_d + m * hp
            sum_v = sum_v + (l + m) * hq
        c = r + ext
        twice, twice_sq = 2.0 * va[r], 2.0 * vsq[c]
        grads[0, r] = twice * (ge[r] * sum_e + gd[r] * sum_d + sum_v)
        grads[1, r] = twice_sq * sum_e
        grads[2, r] = twice_sq * sum_d

    if not coded:
        outs[0][...] = grads[...]
        return
    quarter = ny // 4
    j = lax.axis_index("shot")
    powers = [power_of([grads[n]]) for n in range(3)]
    head = head_row(powers, quarter, offset_ref[0])
    for mask in range(4):
        y0 = pl.multiple_of((j ^ mask) * quarter, quarter)
        for n in range(3):
            part = grads[n, :, pl.ds(y0, quarter)]
            if mask:
                outs[mask][n * rows:(n + 1) * rows] = encoded(part, jnp.exp2(-powers[n]))
            else:
                outs[0][n * rows:(n + 1) * rows] = part
        if mask:
            outs[mask][3 * rows] = head


def gather_kernel(rows, offset_ref, own, *refs):
    codes, (here, *outs), acc = refs[:3], refs[3:7], refs[7]
    around = 4 * rows
    quarter, nz = own.shape[1:]
    zero = jnp.zeros((quarter, nz), jnp.float32)

    @pl.loop(0, around, unroll=8)
    def _(x):
        for n in range(3):
            acc[n, x] = zero

    offset = offset_ref[0]

    for r in range(rows):
        for n in range(3):
            acc[n, lax.rem(r + offset, around)] = own[n * rows + r]

    for code in codes:
        head = code[3 * rows].astype(jnp.int32).astype(jnp.float32)
        theirs = jnp.max(head[8:9]).astype(jnp.int32)
        scales = scales_of(head)
        for n in range(3):
            part = decoded(code[n * rows:(n + 1) * rows], scales[n])
            for r in range(rows):
                acc[n, lax.rem(r + theirs, around)] += part[r]

    here[...] = acc[:, 0:rows].reshape(here.shape)
    for rel in range(1, 4):
        parts = [acc[n, rel * rows:(rel + 1) * rows] for n in range(3)]
        powers = [power_of([part]) for part in parts]
        for n in range(3):
            outs[rel - 1][n * rows:(n + 1) * rows] = encoded(parts[n], jnp.exp2(-powers[n]))
        outs[rel - 1][3 * rows] = head_row(powers, quarter, 0)


def finish_kernel(rows, own, *refs):
    codes, outs = refs[:3], refs[3:]
    scales = [scales_of(code[3 * rows].astype(jnp.int32).astype(jnp.float32)) for code in codes]
    for n in range(3):
        total = own[n * rows:(n + 1) * rows]
        for code, scale in zip(codes, scales):
            total = total + decoded(code[n * rows:(n + 1) * rows], scale[n])
        outs[n][...] = total


def on_device(
    velocity,
    epsilon,
    delta,
    tilt,
    forward_state,
    adjoint_state,
    offsets,
    src_cells,
    rec_cells,
    wavelet,
    observed,
):
    rows, ny, nz = velocity.shape
    tiles = lax.axis_size("tile")
    shots = lax.axis_size("shot")
    steps = wavelet.shape[1]
    ext = 2 * steps - 1
    near = steps - 1
    total = rows + 2 * ext
    span = rows + 2 * near
    assert rows >= ext
    coded = tiles == 4 and shots == 4
    f32, i16 = jnp.float32, jnp.int16

    small = pltpu.CompilerParams(vmem_limit_bytes=4 * 1024 * 1024)

    def struct(*shape, dtype=f32):
        return jax.ShapeDtypeStruct(shape, dtype)

    codes = pl.pallas_call(
        functools.partial(edges_kernel, (ext, steps)),
        out_shape=[struct(2 * (ext + steps), ny, nz, dtype=i16)] * 2,
        in_specs=vmem(2),
        out_specs=vmem(2),
        compiler_params=small,
        cost_estimate=EARLY,
        name="edges",
    )(forward_state, adjoint_state)

    def to_neighbours(up, down):
        return passed_along(up, "tile", 1), passed_along(down, "tile", -1)

    if coded:
        share = lax.select_n(lax.axis_index("shot"), velocity, epsilon, delta, tilt)
        ahead = passed_along(share, "tile", -1)
        behind = passed_along(share, "tile", 1)
        own = jnp.stack([velocity, epsilon, delta, tilt])
        behind, codes, own = lax.optimization_barrier((behind, codes, own))
        ahead, codes = lax.optimization_barrier((ahead, codes))
        across = passed_along(ahead, "tile", -1)
        halo_lo, halo_hi = to_neighbours(*codes)
        far_ahead, far_behind, far_across = (swapped(piece, 2) for piece in (ahead, behind, across))
        model_refs = [own]
        for piece, other in ((ahead, far_ahead), (across, far_across), (behind, far_behind)):
            model_refs += [piece, swapped(piece, 1), other, swapped(other, 1)]
        shift = offsets
    else:
        nbits = max(1, (tiles - 1).bit_length())
        block = jnp.stack([velocity, epsilon, delta, tilt])
        whole = offsets[0] // rows
        for bit in range(nbits):
            moved = passed_along(block, "tile", -(1 << bit))
            block = jnp.where(jnp.bitwise_and(jnp.right_shift(whole, bit), 1) == 1, moved, block)
        model_refs = [block] + [passed_along(block, "tile", -by) for by in (1, 2, -1)]
        halo_lo, halo_hi = to_neighbours(*codes)
        shift = offsets % rows

    field = (total, ny, nz)
    *coefficients, va, ge, gd = pl.pallas_call(
        functools.partial(coefficients_kernel, ext, coded, len(model_refs)),
        out_shape=[struct(*field)] * 5 + [struct(rows, ny, nz)] * 3,
        in_specs=smem(1) + anywhere(len(model_refs)),
        out_specs=vmem(8),
        scratch_shapes=[
            pltpu.VMEM((4, 4, rows, ny // 8, 8, nz), jnp.bfloat16),
            pltpu.SemaphoreType.DMA,
        ],
        compiler_params=pltpu.CompilerParams(vmem_limit_bytes=16 * 1024 * 1024),
        cost_estimate=SHORT,
        name="coefficients",
    )(shift, *map(tiled, model_refs))

    cells, coefficients[0] = lax.optimization_barrier((rec_cells, coefficients[0]))
    dense = pl.pallas_call(
        functools.partial(receivers_kernel, steps, near, rows, tiles),
        out_shape=struct(steps + 1, span, ny, nz),
        in_specs=vmem(2),
        out_specs=pl.BlockSpec(memory_space=pltpu.VMEM),
        compiler_params=pltpu.CompilerParams(vmem_limit_bytes=8 * 1024 * 1024),
        cost_estimate=SHORT,
        name="receivers",
    )(cells, observed)

    kept_h, kept_v, resid = pl.pallas_call(
        functools.partial(forward_kernel, steps, ext, tiles),
        out_shape=[struct(steps, rows, ny, nz)] * 2 + [struct(steps, span, ny, nz)],
        in_specs=smem(2) + vmem(6) + anywhere(3),
        out_specs=vmem(3),
        scratch_shapes=[
            *[pltpu.VMEM((total, ny + 2 * PAD, nz), f32)] * (steps + 1),
            *[pltpu.VMEM(field, f32)] * (steps + 8),
            pltpu.VMEM((2, 2 * ext, ny // 8, 8, nz), i16),
            *[pltpu.SemaphoreType.DMA] * 2,
        ],
        compiler_params=pltpu.CompilerParams(vmem_limit_bytes=32 * 1024 * 1024),
        name="forward",
    )(src_cells, wavelet, *coefficients, dense, forward_state, *map(tiled, (halo_lo, halo_hi)))

    quarter = ny // 4
    if coded:
        wave_outs = [struct(3 * rows, quarter, nz)] + [struct(3 * rows + 1, quarter, nz, dtype=i16)] * 3
    else:
        wave_outs = [struct(3, rows, ny, nz)]
    narrow = (rows + 2 * steps, ny, nz)
    waves = pl.pallas_call(
        functools.partial(adjoint_kernel, steps, ext, coded),
        out_shape=wave_outs,
        in_specs=smem(1) + vmem(11) + anywhere(3),
        out_specs=vmem(len(wave_outs)),
        scratch_shapes=[
            *[pltpu.VMEM(narrow, f32)] * (2 * (steps + 1) + 4),
            pltpu.VMEM((rows + 2 * steps, ny + 2 * PAD, nz), f32),
            pltpu.VMEM(narrow, f32),
            pltpu.VMEM((3, rows, ny, nz), f32),
            pltpu.VMEM((2, 2 * steps, ny // 8, 8, nz), i16),
            *[pltpu.SemaphoreType.DMA] * 2,
        ],
        compiler_params=pltpu.CompilerParams(vmem_limit_bytes=24 * 1024 * 1024),
        name="adjoint",
    )(offsets, *coefficients, va, ge, gd, kept_h, kept_v, resid, adjoint_state, *map(tiled, (halo_lo, halo_hi)))

    if not coded:
        (gradients,) = waves
        within = shift[0]
        spread = jnp.zeros((3, 2 * rows, ny, nz), f32)
        spread = lax.dynamic_update_slice_in_dim(spread, gradients, within, 1)
        combined = spread[:, :rows] + passed_along(spread[:, rows:], "tile", 1)
        for bit in range(nbits):
            moved = passed_along(combined, "tile", 1 << bit)
            combined = jnp.where(jnp.bitwise_and(jnp.right_shift(whole, bit), 1) == 1, moved, combined)
        summed = lax.psum(combined, "shot")
        share = ny // shots
        result = lax.dynamic_slice_in_dim(summed, lax.axis_index("shot") * share, share, 2)
        return (result[0], result[1], result[2])

    own, *sent = waves
    received = [swapped(code, mask) for mask, code in zip((1, 2, 3), sent)]
    part = struct(3 * rows + 1, quarter, nz, dtype=i16)
    here, *parts = pl.pallas_call(
        functools.partial(gather_kernel, rows),
        out_shape=[jax.ShapeDtypeStruct((3 * rows, quarter, nz), f32), part, part, part],
        in_specs=smem(1) + vmem(4),
        out_specs=vmem(4),
        scratch_shapes=[pltpu.VMEM((3, 4 * rows, quarter, nz), f32)],
        compiler_params=small,
        name="gather",
    )(offsets, own, *received)
    arrived = [passed_along(p, "tile", rel) for rel, p in zip((1, 2, 3), parts)]
    return tuple(
        pl.pallas_call(
            functools.partial(finish_kernel, rows),
            out_shape=[jax.ShapeDtypeStruct((rows, quarter, nz), f32)] * 3,
            in_specs=vmem(4),
            out_specs=vmem(3),
            compiler_params=small,
            name="finish",
        )(here, *arrived)
    )


def solution(mesh):
    placed = (
        P(("groups", "tile"), None, None),
        P(("groups", "tile"), None, None),
        P(("groups", "tile"), None, None),
        P(("groups", "tile"), None, None),
        P(("groups", "shot"), None, "tile", None, None),
        P(("groups", "shot"), None, "tile", None, None),
        P(("groups", "shot")),
        P(("groups", "shot")),
        P(("groups", "shot"), None),
        P(("groups", "shot"), None),
        P(("groups", "shot"), None, None),
    )
    return jax.shard_map(
        on_device,
        mesh=mesh,
        in_specs=placed,
        out_specs=(
            P(("groups", "tile"), "shot", None),
            P(("groups", "tile"), "shot", None),
            P(("groups", "tile"), "shot", None),
        ),
        check_vma=False,
    )
```

```python
import functools

import jax
import jax.numpy as jnp
from jax import lax
from jax.experimental import pallas as pl
from jax.experimental.pallas import tpu as pltpu
from jax.sharding import PartitionSpec as P

TOP = 32767.0
PAD = 8
UNROLL = 4
SHORT = pl.CostEstimate(flops=0, bytes_accessed=1024, transcendentals=0)
EARLY = pl.CostEstimate(flops=0, bytes_accessed=16 * 1024 * 1024, transcendentals=0)
STATE_BOUND = 2.0


def passed_along(x, axis, by):
    count = lax.axis_size(axis)
    return lax.ppermute(x, axis, [(i, (i + by) % count) for i in range(count)])


def swapped(x, mask):
    count = lax.axis_size("shot")
    return lax.ppermute(x, "shot", [(i, i ^ mask) for i in range(count)])


def encoded(x, inverse):
    root = jnp.sqrt(jnp.sqrt(jnp.abs(x) * inverse))
    level = jnp.minimum(root * TOP + 0.5, TOP)
    return jnp.where(x < 0, -level, level).astype(jnp.int32).astype(jnp.int16)


def decoded(code, scale):
    level = code.astype(jnp.int32).astype(jnp.float32) * (1.0 / TOP)
    square = level * level
    value = square * square * scale
    return jnp.where(level < 0, -value, value)


def power_of(blocks):
    top = functools.reduce(jnp.maximum, [jnp.max(jnp.abs(x), axis=0) for x in blocks])
    top = jnp.max(jnp.max(top, axis=0, keepdims=True), axis=1, keepdims=True)
    return jnp.ceil(jnp.log2(jnp.maximum(top, 1e-30))) + 1.0


def head_row(powers, lines, offset):
    line = lax.broadcasted_iota(jnp.int32, (lines, 128), 0)
    head = jnp.full((lines, 128), offset, jnp.int32)
    for n, power in enumerate(powers):
        head = jnp.where(line == n, jnp.broadcast_to(power, (lines, 128)).astype(jnp.int32), head)
    return head.astype(jnp.int16)


def scales_of(head):
    return [jnp.exp2(head[n:n + 1]) for n in range(3)]


def tiled(x):
    return x.reshape(x.shape[:-2] + (x.shape[-2] // 8, 8, x.shape[-1]))


def vmem(count):
    return [pl.BlockSpec(memory_space=pltpu.VMEM)] * count


def smem(count):
    return [pl.BlockSpec(memory_space=pltpu.SMEM)] * count


def anywhere(count):
    return [pl.BlockSpec(memory_space=pl.ANY)] * count


def edges_kernel(widths, fwd, adj, up, down):
    rows = fwd.shape[2]
    n = 0
    for state, width in zip((fwd, adj), widths):
        for field in range(2):
            for i in range(width):
                up[n] = encoded(state[0, field, rows - width + i], 1.0 / STATE_BOUND)
                down[n] = encoded(state[0, field, i], 1.0 / STATE_BOUND)
                n += 1


def receivers_kernel(steps, ext, rows, tiles, rec, observed, out):
    span, ny, nz = out.shape[1:]
    count = rec.shape[1]
    nx = rows * tiles
    first = lax.axis_index("tile") * rows - ext
    cells = rec[...]
    plane = ny * nz
    x = cells // plane - first
    x = jnp.where(x < 0, x + nx, x)
    x = jnp.where(x >= nx, x - nx, x)
    line = x * ny + (cells // nz) % ny
    depth = cells % nz
    hit = lax.broadcasted_iota(jnp.int32, (span * ny, count), 0) == line
    hit = jnp.where(hit, 1.0, 0.0).astype(jnp.bfloat16)
    column = lax.broadcasted_iota(jnp.int32, (nz, count), 0) == depth

    def dense(weights):
        dims = (((1,), (1,)), ((), ()))
        return lax.dot_general(hit, weights, dims, preferred_element_type=jnp.float32).reshape(span, ny, nz)

    out[0] = dense(jnp.where(column, 1.0, 0.0).astype(jnp.bfloat16))
    for k in range(steps):
        rest = jnp.where(column, observed[0, k:k + 1, :], 0.0)
        total = None
        for _ in range(3):
            term = rest.astype(jnp.bfloat16)
            rest = rest - term.astype(jnp.float32)
            total = dense(term) if total is None else total + dense(term)
        out[k + 1] = total


def sin_cos(t):
    u = t * t
    s = 1.0 / 6227020800.0
    for c in (-1.0 / 39916800.0, 1.0 / 362880.0, -1.0 / 5040.0, 1.0 / 120.0, -1.0 / 6.0, 1.0):
        s = s * u + c
    s = s * t
    c = 1.0 / 479001600.0
    for d in (-1.0 / 3628800.0, 1.0 / 40320.0, -1.0 / 720.0, 1.0 / 24.0, -0.5, 1.0):
        c = c * u + d
    return s, c


def coefficients_kernel(ext, coded, n_model, offset_ref, *refs):
    model_refs, (vsq, vge, vgd, s2, sc, va_own, ge_own, gd_own) = refs[:n_model], refs[n_model:n_model + 8]
    model, sem = refs[n_model + 8:]
    rows, ny, nz = va_own.shape
    total = rows + 2 * ext
    copies = []
    if coded:
        j = lax.axis_index("shot")
        for index, ref in enumerate(model_refs):
            if index == 0:
                target = model.at[:, 0]
            else:
                target = model.at[j ^ ((index - 1) % 4), (index - 1) // 4 + 1]
            copies.append(pltpu.make_async_copy(ref, target, sem))
    else:
        for rel, ref in enumerate(model_refs):
            for field in range(4):
                copies.append(pltpu.make_async_copy(ref.at[field], model.at[field, rel], sem))
    for copy in copies:
        copy.start()
    for copy in copies:
        copy.wait()
    offset = offset_ref[0]
    around = rows * 4

    def model_row(n, i):
        at = lax.rem(i - ext + offset + around, around)
        return model[n, lax.div(at, rows), lax.rem(at, rows)].astype(jnp.float32).reshape(ny, nz)

    @pl.loop(1, total - 1, unroll=10)
    def _(i):
        va, eps, dlt, angle = (model_row(n, i) for n in range(4))
        sine, cosine = sin_cos(angle)
        square = va * va
        vsq[i] = square
        vge[i] = square * (1.0 + 2.0 * eps)
        vgd[i] = square * (1.0 + 2.0 * dlt)
        s2[i] = sine * sine
        sc[i] = 0.5 * sine * cosine

    @pl.loop(0, rows, unroll=UNROLL)
    def _(i):
        va_own[i] = model_row(0, i + ext)
        ge_own[i] = 1.0 + 2.0 * model_row(1, i + ext)
        gd_own[i] = 1.0 + 2.0 * model_row(2, i + ext)


class Stencils:
    def __init__(self, ny, nz, sums, slopes):
        self.nz, self.sums, self.slopes = nz, sums, slopes
        self.inner = slice(PAD, PAD + ny)
        self.up_one = slice(PAD - 1, PAD + ny - 1)
        self.down_one = slice(PAD + 1, PAD + ny + 1)
        lane = lax.broadcasted_iota(jnp.int32, (ny, nz), 1)
        self.not_first, self.not_last = lane > 0, lane < nz - 1

    def sum_and_slope(self, row):
        lines = row.shape[0]
        above = jnp.where(self.not_last[:lines], pltpu.roll(row, self.nz - 1, 1), 0.0)
        below = jnp.where(self.not_first[:lines], pltpu.roll(row, 1, 1), 0.0)
        return above + below, above - below

    def store_depth(self, turn, field, where, row):
        self.sums[turn][field][where], self.slopes[turn][field][where] = self.sum_and_slope(row)

    def crossed(self, turn, field, i):
        return self.slopes[turn][field][i + 1] - self.slopes[turn][field][i - 1]

    def flat(self, turn, ref, i, a2, c2, ab):
        side = ref[i - 1, self.inner] + ref[i + 1, self.inner]
        beside = ref[i, self.up_one] + ref[i, self.down_one]
        depth = a2 * self.sums[turn][0][i] - ab * self.crossed(turn, 0, i)
        return (c2 * side + beside - 4.0 * ref[i, self.inner]) + depth

    def steep(self, turn, ref, i, a2, c2, ab):
        side = ref[i - 1] + ref[i + 1]
        return (a2 * side - 2.0 * ref[i]) + (c2 * self.sums[turn][1][i] + ab * self.crossed(turn, 1, i))


def clear_edges(refs, total, ny):
    edge = jnp.zeros((PAD, refs[0].shape[2]), jnp.float32)

    @pl.loop(0, total, unroll=total)
    def _(i):
        for ref in refs:
            ref[i, 0:PAD] = edge
            ref[i, PAD + ny:] = edge


def forward_kernel(steps, ext, tiles, source_ref, wavelet_ref, vsq, vge, vgd, s2, sc, dense, fwd, f_lo, f_hi, *refs):
    it = iter(refs)
    kept_h, kept_v, resid = next(it), next(it), next(it)
    press, shear = ([next(it) for _ in range(count)] for count in (steps + 1, steps))
    sums, slopes = ([[next(it) for _ in range(2)] for _ in range(2)] for _ in range(2))
    code, sem, sem_code = it
    rows, ny, nz = fwd.shape[2:]
    total = rows + 2 * ext
    near = steps - 1
    copies = [
        pltpu.make_async_copy(fwd.at[0, 0], press[0].at[pl.ds(ext, rows), pl.ds(PAD, ny)], sem),
        pltpu.make_async_copy(fwd.at[0, 1], shear[0].at[pl.ds(ext, rows)], sem),
    ]
    code_copies = [
        pltpu.make_async_copy(f_lo.at[pl.ds(0, 2 * ext)], code.at[0], sem_code),
        pltpu.make_async_copy(f_hi.at[pl.ds(0, 2 * ext)], code.at[1], sem_code),
    ]
    for copy in code_copies + copies:
        copy.start()
    clear_edges(press[:steps], total, ny)
    ops = Stencils(ny, nz, sums, slopes)
    inner = ops.inner
    for copy in code_copies:
        copy.wait()

    @pl.loop(0, ext, unroll=7)
    def _(i):
        for side, base in ((0, 0), (1, ext + rows)):
            p = decoded(code[side, i], STATE_BOUND).reshape(ny, nz)
            q = decoded(code[side, ext + i], STATE_BOUND).reshape(ny, nz)
            press[0][base + i, inner] = p
            shear[0][base + i] = q
            ops.store_depth(0, 0, base + i, p)
            ops.store_depth(0, 1, base + i, q)

    for copy in copies:
        copy.wait()

    @pl.loop(ext, ext + rows, unroll=8)
    def _(i):
        ops.store_depth(0, 0, i, press[0][i, inner])
        ops.store_depth(0, 1, i, shear[0][i])

    tile_first = lax.axis_index("tile") * rows
    nx = rows * tiles
    cell = source_ref[0]
    src_row = lax.rem(lax.div(cell, ny * nz) - tile_first + ext + nx, nx)
    src_y = lax.rem(lax.div(cell, nz), ny)
    depth = lax.broadcasted_iota(jnp.int32, (1, nz), 1) - lax.rem(cell, nz)
    src_here, src_above, src_below = depth == 0, depth == -1, depth == 1

    for k in range(steps):
        turn, last = k % 2, k == steps - 1
        p_new, q_new = press[k + 1], None if last else shear[k + 1]

        def one_row(i, keep):
            a2, ab = s2[i], sc[i]
            c2 = 1.0 - a2
            hp = ops.flat(turn, press[k], i, a2, c2, ab)
            hq = ops.steep(turn, shear[k], i, a2, c2, ab)
            if keep:
                kept_h[k, i - ext] = hp
                kept_v[k, i - ext] = hq
            steep_part = vsq[i] * hq
            p = press[k][i, inner]
            p_base = 2.0 * p - press[k - 1][i, inner] if k else p
            p = p_base + (vge[i] * hp + steep_part)
            p_new[i, inner] = p
            if last:
                return
            q = shear[k][i]
            q_base = 2.0 * q - shear[k - 1][i] if k else q
            q = q_base + (vgd[i] * hp + steep_part)
            q_new[i] = q
            ops.store_depth(1 - turn, 0, i, p)
            ops.store_depth(1 - turn, 1, i, q)

        @pl.loop(1 + k, ext, unroll=ext - 1 - k)
        def _(i):
            one_row(i, False)
            one_row(total - 1 - i, False)

        pl.loop(ext, ext + rows, unroll=8)(lambda i: one_row(i, True))

        @pl.when((src_row >= 1 + k) & (src_row < total - 1 - k))
        def _():
            amount = wavelet_ref[0, k]
            here, above, below = (jnp.where(mask, amount, 0.0) for mask in (src_here, src_above, src_below))
            line = pl.ds(src_y, 1)
            p_new[src_row, pl.ds(PAD + src_y, 1)] += here
            if not last:
                q_new[src_row, line] += here
                for field in range(2):
                    sums[1 - turn][field][src_row, line] += above + below
                    slopes[1 - turn][field][src_row, line] += above - below

        @pl.loop(near - k, near + rows + k, unroll=rows + 2 * k)
        def _(r):
            resid[k, r] = dense[0, r] * p_new[r + ext - near, inner] - dense[k + 1, r]


def adjoint_kernel(steps, ext, side, offset_ref, vsq, vge, vgd, s2, sc, va, ge, gd, kept_h, kept_v, resid, adj, a_lo, a_hi, *refs):
    it = iter(refs)
    outs = [next(it) for _ in range(2 if side else 1)]
    lam, mu = ([next(it) for _ in range(steps + 1)] for _ in range(2))
    sums, slopes = ([[next(it) for _ in range(2)]] for _ in range(2))
    w1, w2, grads, code, sem, sem_code = it
    rows, all_lines, nz = adj.shape[2:]
    low_c = ext - steps
    total = rows + 2 * steps
    ny = w2.shape[1]
    j = lax.axis_index("shot")
    half = (j // 2 if side == "near" else 1 - j // 2) if side else 0
    first = pl.multiple_of(half * (all_lines - ny), 8)
    lines = pl.ds(first, ny)
    blocks = pl.ds(half * ((all_lines - ny) // 8), ny // 8)
    copies = [
        pltpu.make_async_copy(adj.at[0, 0, :, lines], lam[0].at[pl.ds(steps, rows)], sem),
        pltpu.make_async_copy(adj.at[0, 1, :, lines], mu[0].at[pl.ds(steps, rows)], sem),
    ]
    code_copies = [
        pltpu.make_async_copy(a_lo.at[pl.ds(2 * ext, 2 * steps), blocks], code.at[0], sem_code),
        pltpu.make_async_copy(a_hi.at[pl.ds(2 * ext, 2 * steps), blocks], code.at[1], sem_code),
    ]
    for copy in code_copies + copies:
        copy.start()
    clear_edges([w1], total, ny)
    ops = Stencils(ny, nz, sums, slopes)
    inner = ops.inner
    for copy in code_copies:
        copy.wait()

    @pl.loop(0, steps, unroll=4)
    def _(i):
        for side, base in ((0, 0), (1, steps + rows)):
            lam[0][base + i] = decoded(code[side, i], STATE_BOUND).reshape(ny, nz)
            mu[0][base + i] = decoded(code[side, steps + i], STATE_BOUND).reshape(ny, nz)

    for copy in copies:
        copy.wait()

    for a in range(steps):
        k = steps - 1 - a

        @pl.loop(a, total - a, unroll=total - 2 * a)
        def _(i):
            l, m = lam[a][i], mu[a][i]
            c = i + low_c
            flat_of = vge[c, lines] * l + vgd[c, lines] * m
            steep_of = vsq[c, lines] * (l + m)
            w1[i, inner] = flat_of
            w2[i] = steep_of
            ops.store_depth(0, 0, i, flat_of)
            ops.store_depth(0, 1, i, steep_of)

        @pl.loop(a + 1, total - a - 1, unroll=total - 2 * a - 2)
        def _(i):
            c = i + low_c
            a2, ab = s2[c, lines], sc[c, lines]
            c2 = 1.0 - a2
            h = ops.flat(0, w1, i, a2, c2, ab)
            v = ops.steep(0, w2, i, a2, c2, ab)
            l, m = lam[a][i], mu[a][i]
            l_base = 2.0 * l - lam[a - 1][i] if a else l
            m_base = 2.0 * m - mu[a - 1][i] if a else m
            lam[a + 1][i] = l_base + h + resid[k, i - 1, lines]
            mu[a + 1][i] = m_base + v

    @pl.loop(0, rows, unroll=8)
    def _(r):
        sum_e = sum_d = sum_v = 0.0
        for k in range(steps):
            l, m = lam[steps - k][r + steps], mu[steps - k][r + steps]
            hp, hq = kept_h[k, r, lines], kept_v[k, r, lines]
            sum_e = sum_e + l * hp
            sum_d = sum_d + m * hp
            sum_v = sum_v + (l + m) * hq
        c = r + ext
        twice, twice_sq = 2.0 * va[r, lines], 2.0 * vsq[c, lines]
        grads[0, r] = twice * (ge[r, lines] * sum_e + gd[r, lines] * sum_d + sum_v)
        grads[1, r] = twice_sq * sum_e
        grads[2, r] = twice_sq * sum_d

    if not side:
        outs[0][...] = grads[...]
        return
    quarter = all_lines // 4
    margin = half * (ny - all_lines // 2)
    valid = pl.ds(pl.multiple_of(margin, 8), all_lines // 2)
    powers = [power_of([grads[n, :, valid]]) for n in range(3)]
    head = head_row(powers, quarter, offset_ref[0])
    for out, mask in zip(outs, (0, 1) if side == "near" else (2, 3)):
        y0 = pl.multiple_of(margin + ((j ^ mask) % 2) * quarter, 8)
        for n in range(3):
            part = grads[n, :, pl.ds(y0, quarter)]
            out[n * rows:(n + 1) * rows] = encoded(part, jnp.exp2(-powers[n])) if mask else part
        if mask:
            out[3 * rows] = head


def add_slab(acc, code, rows):
    head = code[3 * rows].astype(jnp.int32).astype(jnp.float32)
    offset = jnp.max(head[8:9]).astype(jnp.int32)
    scales = scales_of(head)
    for n in range(3):
        part = decoded(code[n * rows:(n + 1) * rows], scales[n])
        for r in range(rows):
            acc[n, lax.rem(r + offset, 4 * rows)] += part[r]


def gather_far_kernel(rows, *refs):
    *codes, acc = refs
    zero = jnp.zeros(acc.shape[2:], jnp.float32)

    @pl.loop(0, acc.shape[1], unroll=8)
    def _(x):
        for n in range(3):
            acc[n, x] = zero

    for code in codes:
        add_slab(acc, code, rows)


def gather_kernel(rows, offset_ref, own, beside, far, here, *refs):
    *outs, acc = refs
    quarter = own.shape[1]

    @pl.loop(0, acc.shape[1], unroll=8)
    def _(x):
        for n in range(3):
            acc[n, x] = far[n, x]

    offset = offset_ref[0]
    for r in range(rows):
        for n in range(3):
            acc[n, lax.rem(r + offset, 4 * rows)] += own[n * rows + r]
    add_slab(acc, beside, rows)

    here[...] = acc[:, 0:rows].reshape(here.shape)
    for rel in range(1, 4):
        parts = [acc[n, rel * rows:(rel + 1) * rows] for n in range(3)]
        powers = [power_of([part]) for part in parts]
        for n in range(3):
            outs[rel - 1][n * rows:(n + 1) * rows] = encoded(parts[n], jnp.exp2(-powers[n]))
        outs[rel - 1][3 * rows] = head_row(powers, quarter, 0)


def finish_kernel(rows, own, *refs):
    codes, outs = refs[:3], refs[3:]
    scales = [scales_of(code[3 * rows].astype(jnp.int32).astype(jnp.float32)) for code in codes]
    for n in range(3):
        total = own[n * rows:(n + 1) * rows]
        for code, scale in zip(codes, scales):
            total = total + decoded(code[n * rows:(n + 1) * rows], scale[n])
        outs[n][...] = total


def on_device(
    velocity,
    epsilon,
    delta,
    tilt,
    forward_state,
    adjoint_state,
    offsets,
    src_cells,
    rec_cells,
    wavelet,
    observed,
):
    rows, ny, nz = velocity.shape
    tiles = lax.axis_size("tile")
    shots = lax.axis_size("shot")
    steps = wavelet.shape[1]
    ext = 2 * steps - 1
    near = steps - 1
    total = rows + 2 * ext
    span = rows + 2 * near
    assert rows >= ext
    coded = tiles == 4 and shots == 4
    f32, i16 = jnp.float32, jnp.int16

    small = pltpu.CompilerParams(vmem_limit_bytes=4 * 1024 * 1024)

    def struct(*shape, dtype=f32):
        return jax.ShapeDtypeStruct(shape, dtype)

    codes = pl.pallas_call(
        functools.partial(edges_kernel, (ext, steps)),
        out_shape=[struct(2 * (ext + steps), ny, nz, dtype=i16)] * 2,
        in_specs=vmem(2),
        out_specs=vmem(2),
        compiler_params=small,
        cost_estimate=EARLY,
        name="edges",
    )(forward_state, adjoint_state)

    def to_neighbours(up, down):
        return passed_along(up, "tile", 1), passed_along(down, "tile", -1)

    if coded:
        share = lax.select_n(lax.axis_index("shot"), velocity, epsilon, delta, tilt)
        ahead = passed_along(share, "tile", -1)
        behind = passed_along(share, "tile", 1)
        own = jnp.stack([velocity, epsilon, delta, tilt])
        behind, codes, own = lax.optimization_barrier((behind, codes, own))
        ahead, codes = lax.optimization_barrier((ahead, codes))
        across = passed_along(ahead, "tile", -1)
        halo_lo, halo_hi = to_neighbours(*codes)
        far_ahead, far_behind, far_across = (swapped(piece, 2) for piece in (ahead, behind, across))
        model_refs = [own]
        for piece, other in ((ahead, far_ahead), (across, far_across), (behind, far_behind)):
            model_refs += [piece, swapped(piece, 1), other, swapped(other, 1)]
        shift = offsets
    else:
        nbits = max(1, (tiles - 1).bit_length())
        block = jnp.stack([velocity, epsilon, delta, tilt])
        whole = offsets[0] // rows
        for bit in range(nbits):
            moved = passed_along(block, "tile", -(1 << bit))
            block = jnp.where(jnp.bitwise_and(jnp.right_shift(whole, bit), 1) == 1, moved, block)
        model_refs = [block] + [passed_along(block, "tile", -by) for by in (1, 2, -1)]
        halo_lo, halo_hi = to_neighbours(*codes)
        shift = offsets % rows

    field = (total, ny, nz)
    *coefficients, va, ge, gd = pl.pallas_call(
        functools.partial(coefficients_kernel, ext, coded, len(model_refs)),
        out_shape=[struct(*field)] * 5 + [struct(rows, ny, nz)] * 3,
        in_specs=smem(1) + anywhere(len(model_refs)),
        out_specs=vmem(8),
        scratch_shapes=[
            pltpu.VMEM((4, 4, rows, ny // 8, 8, nz), jnp.bfloat16),
            pltpu.SemaphoreType.DMA,
        ],
        compiler_params=pltpu.CompilerParams(vmem_limit_bytes=16 * 1024 * 1024),
        cost_estimate=SHORT,
        name="coefficients",
    )(shift, *map(tiled, model_refs))

    cells, coefficients[0] = lax.optimization_barrier((rec_cells, coefficients[0]))
    dense = pl.pallas_call(
        functools.partial(receivers_kernel, steps, near, rows, tiles),
        out_shape=struct(steps + 1, span, ny, nz),
        in_specs=vmem(2),
        out_specs=pl.BlockSpec(memory_space=pltpu.VMEM),
        compiler_params=pltpu.CompilerParams(vmem_limit_bytes=8 * 1024 * 1024),
        cost_estimate=SHORT,
        name="receivers",
    )(cells, observed)

    kept_h, kept_v, resid = pl.pallas_call(
        functools.partial(forward_kernel, steps, ext, tiles),
        out_shape=[struct(steps, rows, ny, nz)] * 2 + [struct(steps, span, ny, nz)],
        in_specs=smem(2) + vmem(6) + anywhere(3),
        out_specs=vmem(3),
        scratch_shapes=[
            *[pltpu.VMEM((total, ny + 2 * PAD, nz), f32)] * (steps + 1),
            *[pltpu.VMEM(field, f32)] * (steps + 8),
            pltpu.VMEM((2, 2 * ext, ny // 8, 8, nz), i16),
            *[pltpu.SemaphoreType.DMA] * 2,
        ],
        compiler_params=pltpu.CompilerParams(vmem_limit_bytes=32 * 1024 * 1024),
        name="forward",
    )(src_cells, wavelet, *coefficients, dense, forward_state, *map(tiled, (halo_lo, halo_hi)))

    quarter = ny // 4
    own_part = struct(3 * rows, quarter, nz)
    slab = struct(3 * rows + 1, quarter, nz, dtype=i16)

    def adjoint(side, out_shape):
        lines = ny // 2 + 8 if side else ny
        narrow = (rows + 2 * steps, lines, nz)
        return pl.pallas_call(
            functools.partial(adjoint_kernel, steps, ext, side),
            out_shape=out_shape,
            in_specs=smem(1) + vmem(11) + anywhere(3),
            out_specs=vmem(len(out_shape)),
            scratch_shapes=[
                *[pltpu.VMEM(narrow, f32)] * (2 * (steps + 1) + 4),
                pltpu.VMEM((rows + 2 * steps, lines + 2 * PAD, nz), f32),
                pltpu.VMEM(narrow, f32),
                pltpu.VMEM((3, rows, lines, nz), f32),
                pltpu.VMEM((2, 2 * steps, lines // 8, 8, nz), i16),
                *[pltpu.SemaphoreType.DMA] * 2,
            ],
            compiler_params=pltpu.CompilerParams(vmem_limit_bytes=24 * 1024 * 1024),
            cost_estimate=EARLY if side == "near" else SHORT,
            name="adjoint",
        )(offsets, *coefficients, va, ge, gd, kept_h, kept_v, resid, adjoint_state, *map(tiled, (halo_lo, halo_hi)))

    if coded:
        sent = adjoint("far", [slab] * 2)
        far = [swapped(code, mask) for mask, code in zip((2, 3), sent)]
        _, kept_h = lax.optimization_barrier((sent[0], kept_h))
        own, beside = adjoint("near", [own_part, slab])
        beside = swapped(beside, 1)
        across = pl.pallas_call(
            functools.partial(gather_far_kernel, rows),
            out_shape=struct(3, 4 * rows, quarter, nz),
            in_specs=vmem(2),
            out_specs=pl.BlockSpec(memory_space=pltpu.VMEM),
            compiler_params=small,
            cost_estimate=EARLY,
            name="gather_far",
        )(*far)
    else:
        waves = adjoint(None, [struct(3, rows, ny, nz)])

    if not coded:
        (gradients,) = waves
        within = shift[0]
        spread = jnp.zeros((3, 2 * rows, ny, nz), f32)
        spread = lax.dynamic_update_slice_in_dim(spread, gradients, within, 1)
        combined = spread[:, :rows] + passed_along(spread[:, rows:], "tile", 1)
        for bit in range(nbits):
            moved = passed_along(combined, "tile", 1 << bit)
            combined = jnp.where(jnp.bitwise_and(jnp.right_shift(whole, bit), 1) == 1, moved, combined)
        summed = lax.psum(combined, "shot")
        share = ny // shots
        result = lax.dynamic_slice_in_dim(summed, lax.axis_index("shot") * share, share, 2)
        return (result[0], result[1], result[2])

    part = struct(3 * rows + 1, quarter, nz, dtype=i16)
    here, *parts = pl.pallas_call(
        functools.partial(gather_kernel, rows),
        out_shape=[jax.ShapeDtypeStruct((3 * rows, quarter, nz), f32), part, part, part],
        in_specs=smem(1) + vmem(3),
        out_specs=vmem(4),
        scratch_shapes=[pltpu.VMEM((3, 4 * rows, quarter, nz), f32)],
        compiler_params=small,
        name="gather",
    )(offsets, own, beside, across)
    arrived = [passed_along(p, "tile", rel) for rel, p in zip((1, 2, 3), parts)]
    return tuple(
        pl.pallas_call(
            functools.partial(finish_kernel, rows),
            out_shape=[jax.ShapeDtypeStruct((rows, quarter, nz), f32)] * 3,
            in_specs=vmem(4),
            out_specs=vmem(3),
            compiler_params=small,
            name="finish",
        )(here, *arrived)
    )


def solution(mesh):
    placed = (
        P(("groups", "tile"), None, None),
        P(("groups", "tile"), None, None),
        P(("groups", "tile"), None, None),
        P(("groups", "tile"), None, None),
        P(("groups", "shot"), None, "tile", None, None),
        P(("groups", "shot"), None, "tile", None, None),
        P(("groups", "shot")),
        P(("groups", "shot")),
        P(("groups", "shot"), None),
        P(("groups", "shot"), None),
        P(("groups", "shot"), None, None),
    )
    return jax.shard_map(
        on_device,
        mesh=mesh,
        in_specs=placed,
        out_specs=(
            P(("groups", "tile"), "shot", None),
            P(("groups", "tile"), "shot", None),
            P(("groups", "tile"), "shot", None),
        ),
        check_vma=False,
    )
```

```python
import functools

import jax
import jax.numpy as jnp
from jax import lax
from jax.experimental import pallas as pl
from jax.experimental.pallas import tpu as pltpu
from jax.sharding import PartitionSpec as P

TOP = 32767.0
PAD = 8
UNROLL = 4
SHORT = pl.CostEstimate(flops=0, bytes_accessed=1024, transcendentals=0)
EARLY = pl.CostEstimate(flops=0, bytes_accessed=16 * 1024 * 1024, transcendentals=0)
STATE_BOUND = 2.0


def passed_along(x, axis, by):
    count = lax.axis_size(axis)
    return lax.ppermute(x, axis, [(i, (i + by) % count) for i in range(count)])


def swapped(x, mask):
    count = lax.axis_size("shot")
    return lax.ppermute(x, "shot", [(i, i ^ mask) for i in range(count)])


def encoded(x, inverse):
    root = jnp.sqrt(jnp.sqrt(jnp.abs(x) * inverse))
    level = jnp.minimum(root * TOP + 0.5, TOP)
    return jnp.where(x < 0, -level, level).astype(jnp.int32).astype(jnp.int16)


def decoded(code, scale):
    level = code.astype(jnp.int32).astype(jnp.float32) * (1.0 / TOP)
    square = level * level
    value = square * square * scale
    return jnp.where(level < 0, -value, value)


def power_of(blocks):
    top = functools.reduce(jnp.maximum, [jnp.max(jnp.abs(x), axis=0) for x in blocks])
    top = jnp.max(jnp.max(top, axis=0, keepdims=True), axis=1, keepdims=True)
    return jnp.ceil(jnp.log2(jnp.maximum(top, 1e-30))) + 1.0


def head_row(powers, lines, offset):
    line = lax.broadcasted_iota(jnp.int32, (lines, 128), 0)
    head = jnp.full((lines, 128), offset, jnp.int32)
    for n, power in enumerate(powers):
        head = jnp.where(line == n, jnp.broadcast_to(power, (lines, 128)).astype(jnp.int32), head)
    return head.astype(jnp.int16)


def scales_of(head):
    return [jnp.exp2(head[n:n + 1]) for n in range(3)]


def tiled(x):
    return x.reshape(x.shape[:-2] + (x.shape[-2] // 8, 8, x.shape[-1]))


def vmem(count):
    return [pl.BlockSpec(memory_space=pltpu.VMEM)] * count


def smem(count):
    return [pl.BlockSpec(memory_space=pltpu.SMEM)] * count


def anywhere(count):
    return [pl.BlockSpec(memory_space=pl.ANY)] * count


def edges_kernel(widths, fwd, adj, up, down):
    rows = fwd.shape[2]
    n = 0
    for state, width in zip((fwd, adj), widths):
        for field in range(2):
            for i in range(width):
                up[n] = encoded(state[0, field, rows - width + i], 1.0 / STATE_BOUND)
                down[n] = encoded(state[0, field, i], 1.0 / STATE_BOUND)
                n += 1


def receivers_kernel(steps, ext, rows, tiles, rec, observed, out):
    span, ny, nz = out.shape[1:]
    count = rec.shape[1]
    nx = rows * tiles
    first = lax.axis_index("tile") * rows - ext
    cells = rec[...]
    plane = ny * nz
    x = cells // plane - first
    x = jnp.where(x < 0, x + nx, x)
    x = jnp.where(x >= nx, x - nx, x)
    line = x * ny + (cells // nz) % ny
    depth = cells % nz
    hit = lax.broadcasted_iota(jnp.int32, (span * ny, count), 0) == line
    hit = jnp.where(hit, 1.0, 0.0).astype(jnp.bfloat16)
    column = lax.broadcasted_iota(jnp.int32, (nz, count), 0) == depth

    def dense(weights):
        dims = (((1,), (1,)), ((), ()))
        return lax.dot_general(hit, weights, dims, preferred_element_type=jnp.float32).reshape(span, ny, nz)

    out[0] = dense(jnp.where(column, 1.0, 0.0).astype(jnp.bfloat16))
    for k in range(steps):
        rest = jnp.where(column, observed[0, k:k + 1, :], 0.0)
        total = None
        for _ in range(3):
            term = rest.astype(jnp.bfloat16)
            rest = rest - term.astype(jnp.float32)
            total = dense(term) if total is None else total + dense(term)
        out[k + 1] = total


def sin_cos(t):
    u = t * t
    s = 1.0 / 6227020800.0
    for c in (-1.0 / 39916800.0, 1.0 / 362880.0, -1.0 / 5040.0, 1.0 / 120.0, -1.0 / 6.0, 1.0):
        s = s * u + c
    s = s * t
    c = 1.0 / 479001600.0
    for d in (-1.0 / 3628800.0, 1.0 / 40320.0, -1.0 / 720.0, 1.0 / 24.0, -0.5, 1.0):
        c = c * u + d
    return s, c


def coefficients_kernel(ext, coded, n_model, offset_ref, *refs):
    model_refs, (vsq, vge, vgd, s2, sc, va_own, ge_own, gd_own) = refs[:n_model], refs[n_model:n_model + 8]
    model, sem = refs[n_model + 8:]
    rows, ny, nz = va_own.shape
    total = rows + 2 * ext
    copies = []
    if coded:
        j = lax.axis_index("shot")
        for index, ref in enumerate(model_refs):
            if index == 0:
                target = model.at[:, 0]
            else:
                target = model.at[j ^ ((index - 1) % 4), (index - 1) // 4 + 1]
            copies.append(pltpu.make_async_copy(ref, target, sem))
    else:
        for rel, ref in enumerate(model_refs):
            for field in range(4):
                copies.append(pltpu.make_async_copy(ref.at[field], model.at[field, rel], sem))
    for copy in copies:
        copy.start()
    for copy in copies:
        copy.wait()
    offset = offset_ref[0]
    around = rows * 4

    def model_row(n, i):
        at = lax.rem(i - ext + offset + around, around)
        return model[n, lax.div(at, rows), lax.rem(at, rows)].astype(jnp.float32).reshape(ny, nz)

    @pl.loop(1, total - 1, unroll=10)
    def _(i):
        va, eps, dlt, angle = (model_row(n, i) for n in range(4))
        sine, cosine = sin_cos(angle)
        square = va * va
        vsq[i] = square
        vge[i] = square * (1.0 + 2.0 * eps)
        vgd[i] = square * (1.0 + 2.0 * dlt)
        s2[i] = sine * sine
        sc[i] = 0.5 * sine * cosine

    @pl.loop(0, rows, unroll=UNROLL)
    def _(i):
        va_own[i] = model_row(0, i + ext)
        ge_own[i] = 1.0 + 2.0 * model_row(1, i + ext)
        gd_own[i] = 1.0 + 2.0 * model_row(2, i + ext)


class Stencils:
    def __init__(self, ny, nz, sums, slopes):
        self.nz, self.sums, self.slopes = nz, sums, slopes
        self.inner = slice(PAD, PAD + ny)
        self.up_one = slice(PAD - 1, PAD + ny - 1)
        self.down_one = slice(PAD + 1, PAD + ny + 1)
        lane = lax.broadcasted_iota(jnp.int32, (ny, nz), 1)
        self.not_first, self.not_last = lane > 0, lane < nz - 1

    def sum_and_slope(self, row):
        lines = row.shape[0]
        above = jnp.where(self.not_last[:lines], pltpu.roll(row, self.nz - 1, 1), 0.0)
        below = jnp.where(self.not_first[:lines], pltpu.roll(row, 1, 1), 0.0)
        return above + below, above - below

    def store_depth(self, turn, field, where, row):
        self.sums[turn][field][where], self.slopes[turn][field][where] = self.sum_and_slope(row)

    def crossed(self, turn, field, i):
        return self.slopes[turn][field][i + 1] - self.slopes[turn][field][i - 1]

    def flat(self, turn, ref, i, a2, c2, ab):
        side = ref[i - 1, self.inner] + ref[i + 1, self.inner]
        beside = ref[i, self.up_one] + ref[i, self.down_one]
        depth = a2 * self.sums[turn][0][i] - ab * self.crossed(turn, 0, i)
        return (c2 * side + beside - 4.0 * ref[i, self.inner]) + depth

    def steep(self, turn, ref, i, a2, c2, ab):
        side = ref[i - 1] + ref[i + 1]
        return (a2 * side - 2.0 * ref[i]) + (c2 * self.sums[turn][1][i] + ab * self.crossed(turn, 1, i))


def clear_edges(refs, total, ny):
    edge = jnp.zeros((PAD, refs[0].shape[2]), jnp.float32)

    @pl.loop(0, total, unroll=total)
    def _(i):
        for ref in refs:
            ref[i, 0:PAD] = edge
            ref[i, PAD + ny:] = edge


def forward_kernel(steps, ext, tiles, source_ref, wavelet_ref, vsq, vge, vgd, s2, sc, dense, fwd, f_lo, f_hi, *refs):
    it = iter(refs)
    kept_h, kept_v, resid = next(it), next(it), next(it)
    press, shear = ([next(it) for _ in range(count)] for count in (steps + 1, steps))
    sums, slopes = ([[next(it) for _ in range(2)] for _ in range(2)] for _ in range(2))
    code, sem, sem_code = it
    rows, ny, nz = fwd.shape[2:]
    total = rows + 2 * ext
    near = steps - 1
    copies = [
        pltpu.make_async_copy(fwd.at[0, 0], press[0].at[pl.ds(ext, rows), pl.ds(PAD, ny)], sem),
        pltpu.make_async_copy(fwd.at[0, 1], shear[0].at[pl.ds(ext, rows)], sem),
    ]
    code_copies = [
        pltpu.make_async_copy(f_lo.at[pl.ds(0, 2 * ext)], code.at[0], sem_code),
        pltpu.make_async_copy(f_hi.at[pl.ds(0, 2 * ext)], code.at[1], sem_code),
    ]
    for copy in code_copies + copies:
        copy.start()
    clear_edges(press[:steps], total, ny)
    ops = Stencils(ny, nz, sums, slopes)
    inner = ops.inner
    for copy in code_copies:
        copy.wait()

    @pl.loop(0, ext, unroll=7)
    def _(i):
        for side, base in ((0, 0), (1, ext + rows)):
            p = decoded(code[side, i], STATE_BOUND).reshape(ny, nz)
            q = decoded(code[side, ext + i], STATE_BOUND).reshape(ny, nz)
            press[0][base + i, inner] = p
            shear[0][base + i] = q
            ops.store_depth(0, 0, base + i, p)
            ops.store_depth(0, 1, base + i, q)

    for copy in copies:
        copy.wait()

    @pl.loop(ext, ext + rows, unroll=8)
    def _(i):
        ops.store_depth(0, 0, i, press[0][i, inner])
        ops.store_depth(0, 1, i, shear[0][i])

    tile_first = lax.axis_index("tile") * rows
    nx = rows * tiles
    cell = source_ref[0]
    src_row = lax.rem(lax.div(cell, ny * nz) - tile_first + ext + nx, nx)
    src_y = lax.rem(lax.div(cell, nz), ny)
    depth = lax.broadcasted_iota(jnp.int32, (1, nz), 1) - lax.rem(cell, nz)
    src_here, src_above, src_below = depth == 0, depth == -1, depth == 1

    for k in range(steps):
        turn, last = k % 2, k == steps - 1
        p_new, q_new = press[k + 1], None if last else shear[k + 1]

        def one_row(i, keep):
            a2, ab = s2[i], sc[i]
            c2 = 1.0 - a2
            hp = ops.flat(turn, press[k], i, a2, c2, ab)
            hq = ops.steep(turn, shear[k], i, a2, c2, ab)
            if keep:
                kept_h[k, i - ext] = hp
                kept_v[k, i - ext] = hq
            steep_part = vsq[i] * hq
            p = press[k][i, inner]
            p_base = 2.0 * p - press[k - 1][i, inner] if k else p
            p = p_base + (vge[i] * hp + steep_part)
            p_new[i, inner] = p
            if last:
                return
            q = shear[k][i]
            q_base = 2.0 * q - shear[k - 1][i] if k else q
            q = q_base + (vgd[i] * hp + steep_part)
            q_new[i] = q
            ops.store_depth(1 - turn, 0, i, p)
            ops.store_depth(1 - turn, 1, i, q)

        @pl.loop(1 + k, ext, unroll=ext - 1 - k)
        def _(i):
            one_row(i, False)
            one_row(total - 1 - i, False)

        pl.loop(ext, ext + rows, unroll=8)(lambda i: one_row(i, True))

        @pl.when((src_row >= 1 + k) & (src_row < total - 1 - k))
        def _():
            amount = wavelet_ref[0, k]
            here, above, below = (jnp.where(mask, amount, 0.0) for mask in (src_here, src_above, src_below))
            line = pl.ds(src_y, 1)
            p_new[src_row, pl.ds(PAD + src_y, 1)] += here
            if not last:
                q_new[src_row, line] += here
                for field in range(2):
                    sums[1 - turn][field][src_row, line] += above + below
                    slopes[1 - turn][field][src_row, line] += above - below

        @pl.loop(near - k, near + rows + k, unroll=rows + 2 * k)
        def _(r):
            resid[k, r] = dense[0, r] * p_new[r + ext - near, inner] - dense[k + 1, r]


def adjoint_kernel(steps, ext, side, offset_ref, vsq, vge, vgd, s2, sc, va, ge, gd, kept_h, kept_v, resid, adj, a_lo, a_hi, *refs):
    it = iter(refs)
    outs = [next(it) for _ in range(2 if side else 1)]
    lam, mu = ([next(it) for _ in range(steps + 1)] for _ in range(2))
    sums, slopes = ([[next(it) for _ in range(2)]] for _ in range(2))
    w1, w2, grads, code, sem, sem_code = it
    rows, all_lines, nz = adj.shape[2:]
    low_c = ext - steps
    total = rows + 2 * steps
    ny = w2.shape[1]
    j = lax.axis_index("shot")
    half = (j // 2 if side == "near" else 1 - j // 2) if side else 0
    first = pl.multiple_of(half * (all_lines - ny), 8)
    lines = pl.ds(first, ny)
    blocks = pl.ds(half * ((all_lines - ny) // 8), ny // 8)
    copies = [
        pltpu.make_async_copy(adj.at[0, 0, :, lines], lam[0].at[pl.ds(steps, rows)], sem),
        pltpu.make_async_copy(adj.at[0, 1, :, lines], mu[0].at[pl.ds(steps, rows)], sem),
    ]
    code_copies = [
        pltpu.make_async_copy(a_lo.at[pl.ds(2 * ext, 2 * steps), blocks], code.at[0], sem_code),
        pltpu.make_async_copy(a_hi.at[pl.ds(2 * ext, 2 * steps), blocks], code.at[1], sem_code),
    ]
    for copy in code_copies + copies:
        copy.start()
    clear_edges([w1], total, ny)
    ops = Stencils(ny, nz, sums, slopes)
    inner = ops.inner
    for copy in code_copies:
        copy.wait()

    @pl.loop(0, steps, unroll=4)
    def _(i):
        for side, base in ((0, 0), (1, steps + rows)):
            lam[0][base + i] = decoded(code[side, i], STATE_BOUND).reshape(ny, nz)
            mu[0][base + i] = decoded(code[side, steps + i], STATE_BOUND).reshape(ny, nz)

    for copy in copies:
        copy.wait()

    for a in range(steps):
        k = steps - 1 - a

        @pl.loop(a, total - a, unroll=total - 2 * a)
        def _(i):
            l, m = lam[a][i], mu[a][i]
            c = i + low_c
            flat_of = vge[c, lines] * l + vgd[c, lines] * m
            steep_of = vsq[c, lines] * (l + m)
            w1[i, inner] = flat_of
            w2[i] = steep_of
            ops.store_depth(0, 0, i, flat_of)
            ops.store_depth(0, 1, i, steep_of)

        @pl.loop(a + 1, total - a - 1, unroll=total - 2 * a - 2)
        def _(i):
            c = i + low_c
            a2, ab = s2[c, lines], sc[c, lines]
            c2 = 1.0 - a2
            h = ops.flat(0, w1, i, a2, c2, ab)
            v = ops.steep(0, w2, i, a2, c2, ab)
            l, m = lam[a][i], mu[a][i]
            l_base = 2.0 * l - lam[a - 1][i] if a else l
            m_base = 2.0 * m - mu[a - 1][i] if a else m
            lam[a + 1][i] = l_base + h + resid[k, i - 1, lines]
            mu[a + 1][i] = m_base + v

    @pl.loop(0, rows, unroll=8)
    def _(r):
        sum_e = sum_d = sum_v = 0.0
        for k in range(steps):
            l, m = lam[steps - k][r + steps], mu[steps - k][r + steps]
            hp, hq = kept_h[k, r, lines], kept_v[k, r, lines]
            sum_e = sum_e + l * hp
            sum_d = sum_d + m * hp
            sum_v = sum_v + (l + m) * hq
        c = r + ext
        twice, twice_sq = 2.0 * va[r, lines], 2.0 * vsq[c, lines]
        grads[0, r] = twice * (ge[r, lines] * sum_e + gd[r, lines] * sum_d + sum_v)
        grads[1, r] = twice_sq * sum_e
        grads[2, r] = twice_sq * sum_d

    if not side:
        outs[0][...] = grads[...]
        return
    quarter = all_lines // 4
    margin = half * (ny - all_lines // 2)
    valid = pl.ds(pl.multiple_of(margin, 8), all_lines // 2)
    powers = [power_of([grads[n, :, valid]]) for n in range(3)]
    head = head_row(powers, quarter, offset_ref[0])
    for out, mask in zip(outs, (0, 1) if side == "near" else (2, 3)):
        y0 = pl.multiple_of(margin + ((j ^ mask) % 2) * quarter, 8)
        for n in range(3):
            part = grads[n, :, pl.ds(y0, quarter)]
            out[n * rows:(n + 1) * rows] = encoded(part, jnp.exp2(-powers[n])) if mask else part
        if mask:
            out[3 * rows] = head


def add_slab(acc, code, rows):
    head = code[3 * rows].astype(jnp.int32).astype(jnp.float32)
    offset = jnp.max(head[8:9]).astype(jnp.int32)
    scales = scales_of(head)
    for n in range(3):
        part = decoded(code[n * rows:(n + 1) * rows], scales[n])
        for r in range(rows):
            acc[n, lax.rem(r + offset, 4 * rows)] += part[r]


def gather_far_kernel(rows, *refs):
    *codes, acc = refs
    zero = jnp.zeros(acc.shape[2:], jnp.float32)

    @pl.loop(0, acc.shape[1], unroll=8)
    def _(x):
        for n in range(3):
            acc[n, x] = zero

    for code in codes:
        add_slab(acc, code, rows)


def gather_kernel(rows, offset_ref, own, beside, far, here, *refs):
    *outs, acc = refs
    quarter = own.shape[1]

    @pl.loop(0, acc.shape[1], unroll=8)
    def _(x):
        for n in range(3):
            acc[n, x] = far[n, x]

    offset = offset_ref[0]
    for r in range(rows):
        for n in range(3):
            acc[n, lax.rem(r + offset, 4 * rows)] += own[n * rows + r]
    add_slab(acc, beside, rows)

    here[...] = acc[:, 0:rows].reshape(here.shape)
    for rel in range(1, 4):
        parts = [acc[n, rel * rows:(rel + 1) * rows] for n in range(3)]
        powers = [power_of([part]) for part in parts]
        for n in range(3):
            outs[rel - 1][n * rows:(n + 1) * rows] = encoded(parts[n], jnp.exp2(-powers[n]))
        outs[rel - 1][3 * rows] = head_row(powers, quarter, 0)


def finish_kernel(rows, own, *refs):
    codes, outs = refs[:3], refs[3:]
    scales = [scales_of(code[3 * rows].astype(jnp.int32).astype(jnp.float32)) for code in codes]
    for n in range(3):
        total = own[n * rows:(n + 1) * rows]
        for code, scale in zip(codes, scales):
            total = total + decoded(code[n * rows:(n + 1) * rows], scale[n])
        outs[n][...] = total


def on_device(
    velocity,
    epsilon,
    delta,
    tilt,
    forward_state,
    adjoint_state,
    offsets,
    src_cells,
    rec_cells,
    wavelet,
    observed,
):
    rows, ny, nz = velocity.shape
    tiles = lax.axis_size("tile")
    shots = lax.axis_size("shot")
    steps = wavelet.shape[1]
    ext = 2 * steps - 1
    near = steps - 1
    total = rows + 2 * ext
    span = rows + 2 * near
    assert rows >= ext
    coded = tiles == 4 and shots == 4
    f32, i16 = jnp.float32, jnp.int16

    small = pltpu.CompilerParams(vmem_limit_bytes=4 * 1024 * 1024)

    def struct(*shape, dtype=f32):
        return jax.ShapeDtypeStruct(shape, dtype)

    codes = pl.pallas_call(
        functools.partial(edges_kernel, (ext, steps)),
        out_shape=[struct(2 * (ext + steps), ny, nz, dtype=i16)] * 2,
        in_specs=vmem(2),
        out_specs=vmem(2),
        compiler_params=small,
        cost_estimate=EARLY,
        name="edges",
    )(forward_state, adjoint_state)

    def to_neighbours(up, down):
        return passed_along(up, "tile", 1), passed_along(down, "tile", -1)

    if coded:
        share = lax.select_n(lax.axis_index("shot"), velocity, epsilon, delta, tilt)
        ahead = passed_along(share, "tile", -1)
        behind = passed_along(share, "tile", 1)
        own = jnp.stack([velocity, epsilon, delta, tilt])
        behind, codes, own = lax.optimization_barrier((behind, codes, own))
        ahead, codes = lax.optimization_barrier((ahead, codes))
        across = passed_along(ahead, "tile", -1)
        halo_lo, halo_hi = to_neighbours(*codes)
        far_ahead, far_behind, far_across = (swapped(piece, 2) for piece in (ahead, behind, across))
        model_refs = [own]
        for piece, other in ((ahead, far_ahead), (across, far_across), (behind, far_behind)):
            model_refs += [piece, swapped(piece, 1), other, swapped(other, 1)]
        shift = offsets
    else:
        nbits = max(1, (tiles - 1).bit_length())
        block = jnp.stack([velocity, epsilon, delta, tilt])
        whole = offsets[0] // rows
        for bit in range(nbits):
            moved = passed_along(block, "tile", -(1 << bit))
            block = jnp.where(jnp.bitwise_and(jnp.right_shift(whole, bit), 1) == 1, moved, block)
        model_refs = [block] + [passed_along(block, "tile", -by) for by in (1, 2, -1)]
        halo_lo, halo_hi = to_neighbours(*codes)
        shift = offsets % rows

    field = (total, ny, nz)
    *coefficients, va, ge, gd = pl.pallas_call(
        functools.partial(coefficients_kernel, ext, coded, len(model_refs)),
        out_shape=[struct(*field)] * 5 + [struct(rows, ny, nz)] * 3,
        in_specs=smem(1) + anywhere(len(model_refs)),
        out_specs=vmem(8),
        scratch_shapes=[
            pltpu.VMEM((4, 4, rows, ny // 8, 8, nz), jnp.bfloat16),
            pltpu.SemaphoreType.DMA,
        ],
        compiler_params=pltpu.CompilerParams(vmem_limit_bytes=46 * 1024 * 1024),
        cost_estimate=SHORT,
        name="coefficients",
    )(shift, *map(tiled, model_refs))

    cells, coefficients[0] = lax.optimization_barrier((rec_cells, coefficients[0]))
    dense = pl.pallas_call(
        functools.partial(receivers_kernel, steps, near, rows, tiles),
        out_shape=struct(steps + 1, span, ny, nz),
        in_specs=vmem(2),
        out_specs=pl.BlockSpec(memory_space=pltpu.VMEM),
        compiler_params=pltpu.CompilerParams(vmem_limit_bytes=8 * 1024 * 1024),
        cost_estimate=SHORT,
        name="receivers",
    )(cells, observed)

    kept_h, kept_v, resid = pl.pallas_call(
        functools.partial(forward_kernel, steps, ext, tiles),
        out_shape=[struct(steps, rows, ny, nz)] * 2 + [struct(steps, span, ny, nz)],
        in_specs=smem(2) + vmem(6) + anywhere(3),
        out_specs=vmem(3),
        scratch_shapes=[
            *[pltpu.VMEM((total, ny + 2 * PAD, nz), f32)] * (steps + 1),
            *[pltpu.VMEM(field, f32)] * (steps + 8),
            pltpu.VMEM((2, 2 * ext, ny // 8, 8, nz), i16),
            *[pltpu.SemaphoreType.DMA] * 2,
        ],
        compiler_params=pltpu.CompilerParams(vmem_limit_bytes=32 * 1024 * 1024),
        name="forward",
    )(src_cells, wavelet, *coefficients, dense, forward_state, *map(tiled, (halo_lo, halo_hi)))

    quarter = ny // 4
    own_part = struct(3 * rows, quarter, nz)
    slab = struct(3 * rows + 1, quarter, nz, dtype=i16)

    def adjoint(side, out_shape):
        lines = ny // 2 + 8 if side else ny
        narrow = (rows + 2 * steps, lines, nz)
        return pl.pallas_call(
            functools.partial(adjoint_kernel, steps, ext, side),
            out_shape=out_shape,
            in_specs=smem(1) + vmem(11) + anywhere(3),
            out_specs=vmem(len(out_shape)),
            scratch_shapes=[
                *[pltpu.VMEM(narrow, f32)] * (2 * (steps + 1) + 4),
                pltpu.VMEM((rows + 2 * steps, lines + 2 * PAD, nz), f32),
                pltpu.VMEM(narrow, f32),
                pltpu.VMEM((3, rows, lines, nz), f32),
                pltpu.VMEM((2, 2 * steps, lines // 8, 8, nz), i16),
                *[pltpu.SemaphoreType.DMA] * 2,
            ],
            compiler_params=pltpu.CompilerParams(vmem_limit_bytes=24 * 1024 * 1024),
            cost_estimate=EARLY if side == "near" else SHORT,
            name="adjoint",
        )(offsets, *coefficients, va, ge, gd, kept_h, kept_v, resid, adjoint_state, *map(tiled, (halo_lo, halo_hi)))

    if coded:
        sent = adjoint("far", [slab] * 2)
        far = [swapped(code, mask) for mask, code in zip((2, 3), sent)]
        _, kept_h = lax.optimization_barrier((sent[0], kept_h))
        own, beside = adjoint("near", [own_part, slab])
        beside = swapped(beside, 1)
        across = pl.pallas_call(
            functools.partial(gather_far_kernel, rows),
            out_shape=struct(3, 4 * rows, quarter, nz),
            in_specs=vmem(2),
            out_specs=pl.BlockSpec(memory_space=pltpu.VMEM),
            compiler_params=small,
            cost_estimate=EARLY,
            name="gather_far",
        )(*far)
    else:
        waves = adjoint(None, [struct(3, rows, ny, nz)])

    if not coded:
        (gradients,) = waves
        within = shift[0]
        spread = jnp.zeros((3, 2 * rows, ny, nz), f32)
        spread = lax.dynamic_update_slice_in_dim(spread, gradients, within, 1)
        combined = spread[:, :rows] + passed_along(spread[:, rows:], "tile", 1)
        for bit in range(nbits):
            moved = passed_along(combined, "tile", 1 << bit)
            combined = jnp.where(jnp.bitwise_and(jnp.right_shift(whole, bit), 1) == 1, moved, combined)
        summed = lax.psum(combined, "shot")
        share = ny // shots
        result = lax.dynamic_slice_in_dim(summed, lax.axis_index("shot") * share, share, 2)
        return (result[0], result[1], result[2])

    part = struct(3 * rows + 1, quarter, nz, dtype=i16)
    here, *parts = pl.pallas_call(
        functools.partial(gather_kernel, rows),
        out_shape=[jax.ShapeDtypeStruct((3 * rows, quarter, nz), f32), part, part, part],
        in_specs=smem(1) + vmem(3),
        out_specs=vmem(4),
        scratch_shapes=[pltpu.VMEM((3, 4 * rows, quarter, nz), f32)],
        compiler_params=small,
        name="gather",
    )(offsets, own, beside, across)
    arrived = [passed_along(p, "tile", rel) for rel, p in zip((1, 2, 3), parts)]
    return tuple(
        pl.pallas_call(
            functools.partial(finish_kernel, rows),
            out_shape=[jax.ShapeDtypeStruct((rows, quarter, nz), f32)] * 3,
            in_specs=vmem(4),
            out_specs=vmem(3),
            compiler_params=small,
            name="finish",
        )(here, *arrived)
    )


def solution(mesh):
    placed = (
        P(("groups", "tile"), None, None),
        P(("groups", "tile"), None, None),
        P(("groups", "tile"), None, None),
        P(("groups", "tile"), None, None),
        P(("groups", "shot"), None, "tile", None, None),
        P(("groups", "shot"), None, "tile", None, None),
        P(("groups", "shot")),
        P(("groups", "shot")),
        P(("groups", "shot"), None),
        P(("groups", "shot"), None),
        P(("groups", "shot"), None, None),
    )
    return jax.shard_map(
        on_device,
        mesh=mesh,
        in_specs=placed,
        out_specs=(
            P(("groups", "tile"), "shot", None),
            P(("groups", "tile"), "shot", None),
            P(("groups", "tile"), "shot", None),
        ),
        check_vma=False,
    )
```
